32 devices in a mesh: dp: 32 (over z, y, x, core).
Axes of the slice: x: 2, y: 2, z: 4, core: 2. Of those that a mesh axis runs over, the one named last changes fastest.
Arguments:
- gradient: float32 [32, 4096, 128], P('dp'), may hold values from -6 to 6
- residual: float32 [32, 4096, 128], P('dp'), may hold values from -5 to 5
- weights: float32 [4096, 128], replicated, may hold values from -6 to 6
- momentum: float32 [4096, 128], replicated, may hold values from -6 to 6
- sel_idx: int32 [32, 32, 4], replicated, may hold values from 0 to 4095, as said below
- sel_count: int32 [32, 32], replicated, may hold values from 1 to 4, as said below
- gath_idx: int32 [32, 8], replicated, may hold values from 0 to 4095, as said below
- gath_count: int32 [32], replicated, may hold values from 6 to 8, as said below
Outputs:
- new_weights: float32 [4096, 128], replicated
- new_momentum: float32 [4096, 128], replicated
- new_residual: float32 [32, 4096, 128], P('dp')
The draws below stay inside these ranges and needn't reach their ends.
Inputs may be any that keep to these rules, and one draw needn't show every extreme that they name: Owners' regions are consecutive runs of blocks in owner order covering all 4096 blocks, each of 64 to 192 blocks, some of exactly 192. All 4 entries of sel_idx[s, o] are distinct entries of gath_idx[o], those at or beyond sel_count[s, o] included. `sel_count`: some owner receives exactly 4 used slots from every replica. All 8 entries of gath_idx[o] are distinct blocks of owner o's region. `gath_count`: some owner lists exactly 8 blocks.
All inputs are finite; a program needn't handle non-finite values.
Results may differ from the reference program's by a relative error of at most 0.00002.
Values sent between devices are 32-bit elements; how exact they have to be, the bound alone decides.
A program may use at most 192 MiB of HBM per device.

```python
import jax
import jax.numpy as jnp
from jax import lax

BLK = 128
BLK_OWN = 128
CAP = 4
GCAP = 8
NBLK = 4096
N_DP = 32


def make_lists(key):
    base_key = jax.random.fold_in(key, 7177)
    keys = jax.random.split(base_key, 9)
    half_len = BLK_OWN // 2
    pair_count = N_DP // 2
    longest = BLK_OWN + half_len
    deltas = jax.random.randint(keys[0], (pair_count,), 0, half_len + 1)
    forced = jax.random.randint(keys[1], (), 0, pair_count)
    deltas = deltas.at[forced].set(half_len)
    lengths = jnp.concatenate([BLK_OWN + deltas, BLK_OWN - deltas]).astype(jnp.int32)
    lengths = jax.random.permutation(keys[2], lengths)
    starts = jnp.cumsum(lengths) - lengths
    positions = jnp.arange(longest, dtype=jnp.int32)
    gath_scores = jax.random.randint(keys[6], (N_DP, longest), 0, 65536) * longest + positions
    gath_scores = jnp.where(positions[None, :] < lengths[:, None], gath_scores, -1)
    gath_offsets = lax.top_k(gath_scores, GCAP)[1]
    gath_idx = (starts[:, None] + gath_offsets).astype(jnp.int32)
    low_count = GCAP - GCAP // 4
    gath_count = jax.random.randint(keys[7], (N_DP,), low_count, GCAP + 1)
    full_lister = jax.random.randint(keys[8], (), 0, N_DP)
    gath_count = gath_count.at[(full_lister + 1) % N_DP].set(low_count)
    gath_count = gath_count.at[full_lister].set(GCAP).astype(jnp.int32)
    list_pos = jnp.arange(GCAP, dtype=jnp.int32)
    sel_scores = jax.random.randint(keys[3], (N_DP, N_DP, GCAP), 0, 65536) * GCAP + list_pos
    sel_pick = lax.top_k(sel_scores, CAP)[1]
    gath_wide = jnp.broadcast_to(gath_idx[None, :, :], (N_DP, N_DP, GCAP))
    sel_idx = jnp.take_along_axis(gath_wide, sel_pick, axis=2).astype(jnp.int32)
    sel_count = jax.random.randint(keys[4], (N_DP, N_DP), 1, CAP + 1)
    full_owner = jax.random.randint(keys[5], (), 0, N_DP)
    sel_count = sel_count.at[:, full_owner].set(CAP).astype(jnp.int32)
    return (sel_idx, sel_count, gath_idx, gath_count)


def draw_sel_idx(key, part):
    return make_lists(key)[0]


def draw_sel_count(key, part):
    return make_lists(key)[1]


def draw_gath_idx(key, part):
    return make_lists(key)[2]


def draw_gath_count(key, part):
    return make_lists(key)[3]


def level_of(key, extent, shards, low, top_value):
    factor_of, own = 1.0, jax.random.fold_in(key, 6)
    for position, shards_of in shards:
        steps = jnp.exp(jax.random.uniform(jax.random.fold_in(own, position), (shards_of,), jnp.float32, low / len(shards), top_value / len(shards)))
        factor_of = factor_of * jnp.repeat(steps, extent[position] // shards_of).reshape([-1 if axis == position else 1 for axis in range(len(extent))])
    return factor_of


def normal_values(stream_key, extent, deviation, reach, pieces=(), held_as=jnp.bfloat16):
    values = jax.random.normal(stream_key, extent, jnp.float32) * deviation
    if len(pieces) > 0:
        values = level_of(stream_key, extent, pieces, -0.22, 0.18) * values
    return jnp.clip(values, min=-reach, max=reach).astype(held_as)


def setup_inputs(seed: int = 0) -> dict:
    arg_keys = jax.random.split(jax.random.key(seed), 9)
    gradient = normal_values(arg_keys[0], (N_DP, NBLK, BLK), 1.0, 6.0, ((0, 32),), jnp.float32)
    residual = normal_values(arg_keys[1], (N_DP, NBLK, BLK), 0.7, 5.0, ((0, 32),), jnp.float32)
    weights = normal_values(arg_keys[2], (NBLK, BLK), 1.0, 6.0, (), jnp.float32)
    momentum = normal_values(arg_keys[3], (NBLK, BLK), 1.0, 6.0, (), jnp.float32)
    sel_idx = draw_sel_idx(jax.random.fold_in(arg_keys[8], 71), 0)
    sel_count = draw_sel_count(jax.random.fold_in(arg_keys[8], 71), 0)
    gath_idx = draw_gath_idx(jax.random.fold_in(arg_keys[8], 71), 0)
    gath_count = draw_gath_count(jax.random.fold_in(arg_keys[8], 71), 0)
    return {"gradient": gradient, "residual": residual, "weights": weights, "momentum": momentum, "sel_idx": sel_idx, "sel_count": sel_count, "gath_idx": gath_idx, "gath_count": gath_count}


momentum_coef = 0.9
learning_rate = 0.05


def reference(gradient, residual, weights, momentum, sel_idx, sel_count, gath_idx, gath_count):
    accumulated = gradient + residual
    slot_ids = jnp.arange(CAP, dtype=jnp.int32)
    sel_valid = (slot_ids[None, None, :] < sel_count[:, :, None]).astype(jnp.float32)

    def add_source(running, inputs):
        source_acc, source_ids, source_valid = inputs
        flat_ids = source_ids.reshape(-1)
        rows_in = source_acc[flat_ids] * source_valid.reshape(-1, 1)
        return running.at[flat_ids].add(rows_in), None

    summed = lax.scan(add_source, jnp.zeros((NBLK, BLK), jnp.float32), (accumulated, sel_idx, sel_valid))[0]
    gath_slots = jnp.arange(GCAP, dtype=jnp.int32)
    gath_valid = (gath_slots[None, :] < gath_count[:, None]).astype(jnp.float32)
    listed = jnp.zeros((NBLK,), jnp.float32).at[gath_idx.reshape(-1)].max(gath_valid.reshape(-1))
    update = summed * listed[:, None]
    new_momentum = momentum_coef * momentum + update
    new_weights = weights - learning_rate * new_momentum

    def source_mask(source_ids, source_valid):
        return jnp.zeros((NBLK,), jnp.float32).at[source_ids.reshape(-1)].max(source_valid.reshape(-1))

    sel_mask = jax.vmap(source_mask)(sel_idx, sel_valid)
    new_residual = accumulated * (1.0 - sel_mask * listed[None, :])[:, :, None]
    return new_weights, new_momentum, new_residual
```

```python
import functools

import jax
import jax.numpy as jnp
from jax import lax
from jax.experimental import pallas as pl
from jax.experimental.pallas import tpu as pltpu
from jax.sharding import PartitionSpec as P

MESH = pl.DeviceIdType.MESH
momentum_coef = 0.9
learning_rate = 0.05
ROWS = 8


def exchange(
    n, chunk,
    grad, resid, weights, momentum, sel, counts, lists, list_counts,
    acc, mom, wts, kept, mrows, wrows, ids,
    res_buf, sel_s, cnt_s, gcnt_s, flags, outgoing, incoming, updates,
    load_sem, table_sem, send_sem, recv_sem, send2_sem, recv2_sem,
):
    me = lax.axis_index("dp")
    cap, list_len = sel_s.shape[0], ids.shape[0]
    block_count = acc.shape[0]

    band = pl.multiple_of((me // ROWS) * ROWS, ROWS)
    tables = [
        pltpu.make_async_copy(lists, ids, table_sem.at[0]),
        pltpu.make_async_copy(sel.at[me], sel_s, table_sem.at[1]),
        pltpu.make_async_copy(counts.at[pl.ds(band, ROWS)], cnt_s, table_sem.at[2]),
        pltpu.make_async_copy(list_counts, gcnt_s, table_sem.at[3]),
    ]
    loads = [
        pltpu.make_async_copy(grad, acc, load_sem.at[0]),
        pltpu.make_async_copy(resid, res_buf, load_sem.at[1]),
        pltpu.make_async_copy(momentum, mom, load_sem.at[2]),
        pltpu.make_async_copy(weights, wts, load_sem.at[3]),
    ]
    for copy in tables + loads:
        copy.start()

    barrier = pltpu.get_barrier_semaphore()

    def greet(k, _):
        pl.semaphore_signal(barrier, inc=1, device_id=(lax.rem(me + k, n),), device_id_type=MESH)
        return 0

    lax.fori_loop(1, n, greet, 0)

    for copy in tables:
        copy.wait()
    my_row = me - band

    def flag_owner(o, _):
        used = cnt_s[my_row, o]
        listed = gcnt_s[o]
        picks = [jnp.where(c < used, sel_s[c, o], -1) for c in range(cap)]
        for j in range(list_len):
            block = ids[j, o]
            hit = picks[0] == block
            for pick in picks[1:]:
                hit = jnp.logical_or(hit, pick == block)
            hit = jnp.logical_and(hit, j < listed)
            flags[j, o] = jnp.where(hit, jnp.float32(1.0), jnp.float32(0.0))
        return 0

    lax.fori_loop(0, n, flag_owner, 0)

    loads[0].wait()
    loads[1].wait()
    pl.semaphore_wait(barrier, n - 1)

    def pick_rows(o, target):
        for j in range(list_len):
            block = ids[j, o]
            row = acc[pl.ds(block, 1), :] + res_buf[pl.ds(block, 1), :]
            sent = row * flags[j, o]
            outgoing[o, pl.ds(j, 1), :] = sent
            if target is not None:
                target[o, pl.ds(j, 1), :] = sent
            kept[o, pl.ds(j, 1), :] = row - sent

    def send_to_owner(k, _):
        o = lax.rem(me + k, n)
        pick_rows(o, None)
        pltpu.make_async_remote_copy(
            src_ref=outgoing.at[o], dst_ref=incoming.at[me],
            send_sem=send_sem, recv_sem=recv_sem,
            device_id=(o,), device_id_type=MESH,
        ).start()
        return 0

    lax.fori_loop(1, n, send_to_owner, 0)
    pick_rows(me, incoming)

    def all_of(buffer, send, recv):
        part = buffer.at[pl.ds(0, n - 1)]
        return pltpu.make_async_remote_copy(
            src_ref=part, dst_ref=part, send_sem=send, recv_sem=recv,
            device_id=(lax.rem(me + 1, n),), device_id_type=MESH,
        )

    loads[2].wait()
    loads[3].wait()

    def pick_weights(o, _):
        for j in range(list_len):
            wrows[o, pl.ds(j, 1), :] = wts[pl.ds(ids[j, o], 1), :]
        return 0

    lax.fori_loop(0, n, pick_weights, 0)

    def dense_step(i, _):
        rows = pl.ds(pl.multiple_of(i * chunk, chunk), chunk)
        decayed = momentum_coef * mom[rows, :]
        mom[rows, :] = decayed
        wts[rows, :] = wts[rows, :] - learning_rate * decayed
        return 0

    lax.fori_loop(0, block_count // chunk, dense_step, 0)

    all_of(incoming, send_sem, recv_sem).wait_recv()
    updates[me] = jnp.sum(incoming[...], axis=0)

    def send_sum(k, _):
        pltpu.make_async_remote_copy(
            src_ref=updates.at[me], dst_ref=updates.at[me],
            send_sem=send2_sem, recv_sem=recv2_sem,
            device_id=(lax.rem(me + k, n),), device_id_type=MESH,
        ).start()
        return 0

    lax.fori_loop(1, n, send_sum, 0)

    def dense_acc(i, _):
        rows = pl.ds(pl.multiple_of(i * chunk, chunk), chunk)
        acc[rows, :] = acc[rows, :] + res_buf[rows, :]
        return 0

    lax.fori_loop(0, block_count // chunk, dense_acc, 0)

    def pick_momentum(o, _):
        for j in range(list_len):
            mrows[o, pl.ds(j, 1), :] = mom[pl.ds(ids[j, o], 1), :]
        return 0

    lax.fori_loop(0, n, pick_momentum, 0)

    all_of(outgoing, send_sem, recv_sem).wait_send()
    all_of(updates, send2_sem, recv2_sem).wait_recv()
    new_rows = mrows[...] + updates[...]
    mrows[...] = new_rows
    wrows[...] = wrows[...] - learning_rate * new_rows
    all_of(updates, send2_sem, recv2_sem).wait_send()


def finish(
    ids, acc_in, mom_in, wts_in, kept, mrows, wrows,
    new_weights, new_momentum, new_residual, acc, mom, wts,
    sems,
):
    n, list_len = kept.shape[0], kept.shape[1]
    copies = []
    for i, (rows, whole, result) in enumerate(
        ((kept, acc, new_residual), (mrows, mom, new_momentum), (wrows, wts, new_weights))
    ):
        def place(o, _, rows=rows, whole=whole):
            tile = rows[o]
            for j in range(list_len):
                whole[pl.ds(ids[j, o], 1), :] = tile[j:j + 1]
            return 0

        lax.fori_loop(0, n, place, 0)
        copies.append(pltpu.make_async_copy(whole, result, sems.at[i]))
        copies[-1].start()
    for copy in copies:
        copy.wait()


def local(n, gradient, residual, weights, momentum, sel_idx, sel_count, gath_idx, gath_count):
    block_count, block_len = weights.shape
    cap, list_len = sel_idx.shape[2], gath_idx.shape[1]
    f32, i32 = jnp.float32, jnp.int32
    dense = pltpu.VMEM((block_count, block_len), f32)
    tiles = pltpu.VMEM((n, list_len, block_len), f32)
    table = pltpu.SMEM((list_len, n), i32)
    any_space = pl.BlockSpec(memory_space=pl.ANY)
    vmem = pl.BlockSpec(memory_space=pltpu.VMEM)
    smem = pl.BlockSpec(memory_space=pltpu.SMEM)
    dense_bytes = block_count * block_len * 4
    tile_bytes = n * list_len * block_len * 4
    chunk = 64

    acc, mom, wts, kept, mrows, wrows, ids = pl.pallas_call(
        functools.partial(exchange, n, chunk),
        out_shape=(dense, dense, dense, tiles, tiles, tiles, table),
        in_specs=[any_space] * 8,
        out_specs=[vmem] * 6 + [smem],
        scratch_shapes=[
            dense,
            pltpu.SMEM((cap, n), i32),
            pltpu.SMEM((ROWS, n), i32),
            pltpu.SMEM((n,), i32),
            pltpu.SMEM((list_len, n), f32),
            tiles,
            tiles,
            tiles,
            pltpu.SemaphoreType.DMA((4,)),
            pltpu.SemaphoreType.DMA((4,)),
            pltpu.SemaphoreType.DMA,
            pltpu.SemaphoreType.DMA,
            pltpu.SemaphoreType.DMA,
            pltpu.SemaphoreType.DMA,
        ],
        compiler_params=pltpu.CompilerParams(
            collective_id=0, has_side_effects=True,
            vmem_limit_bytes=dense_bytes + 4 * tile_bytes + (1 << 21),
        ),
        cost_estimate=pl.CostEstimate(
            flops=5 * block_count * block_len, bytes_accessed=4 * dense_bytes, transcendentals=0
        ),
        name="exchange",
    )(
        gradient.reshape(block_count, block_len),
        residual.reshape(block_count, block_len),
        weights,
        momentum,
        sel_idx.transpose(0, 2, 1),
        sel_count,
        gath_idx.T,
        gath_count,
    )
    whole = jax.ShapeDtypeStruct((block_count, block_len), f32)
    new_weights, new_momentum, new_residual, _, _, _ = pl.pallas_call(
        finish,
        out_shape=(whole, whole, whole, dense, dense, dense),
        in_specs=[smem] + [vmem] * 6,
        out_specs=[any_space] * 3 + [vmem] * 3,
        input_output_aliases={1: 3, 2: 4, 3: 5},
        scratch_shapes=[pltpu.SemaphoreType.DMA((3,))],
        compiler_params=pltpu.CompilerParams(vmem_limit_bytes=1 << 21),
        cost_estimate=pl.CostEstimate(flops=0, bytes_accessed=3 * dense_bytes, transcendentals=0),
        name="finish",
    )(ids, acc, mom, wts, kept, mrows, wrows)
    return new_weights, new_momentum, new_residual[None]


def solution(mesh):
    placed = (P("dp", None, None), P("dp", None, None), P(), P(), P(), P(), P(), P())
    return jax.shard_map(
        functools.partial(local, mesh.shape["dp"]),
        mesh=mesh,
        in_specs=placed,
        out_specs=(P(), P(), P("dp", None, None)),
        check_vma=False,
    )
```

```python
import functools

import jax
import jax.numpy as jnp
from jax import lax
from jax.experimental import pallas as pl
from jax.experimental.pallas import tpu as pltpu
from jax.sharding import PartitionSpec as P

MESH = pl.DeviceIdType.MESH
momentum_coef = 0.9
learning_rate = 0.05
ROWS = 8
PIECES = 2


def pieces(source, target, sems, first):
    rows = source.shape[0] // PIECES
    return [
        pltpu.make_async_copy(
            source.at[pl.ds(i * rows, rows)], target.at[pl.ds(i * rows, rows)], sems.at[first + i]
        )
        for i in range(PIECES)
    ]


def exchange(
    n, chunk,
    grad, resid, weights, momentum, sel, counts, lists, list_counts,
    acc, mom, wts, kept, mrows, wrows, ids,
    res_buf, sel_s, cnt_s, gcnt_s, flags, outgoing, incoming, updates,
    load_sem, table_sem, send_sem, recv_sem, send2_sem, recv2_sem,
):
    me = lax.axis_index("dp")
    cap, list_len = sel_s.shape[0], ids.shape[0]
    block_count = acc.shape[0]

    band = pl.multiple_of((me // ROWS) * ROWS, ROWS)
    tables = [
        pltpu.make_async_copy(lists, ids, table_sem.at[0]),
        pltpu.make_async_copy(sel.at[me], sel_s, table_sem.at[1]),
        pltpu.make_async_copy(counts.at[pl.ds(band, ROWS)], cnt_s, table_sem.at[2]),
        pltpu.make_async_copy(list_counts, gcnt_s, table_sem.at[3]),
    ]

    def load(source, target, first):
        return pieces(source, target, load_sem, first)

    first_loads = load(grad, acc, 0) + load(resid, res_buf, PIECES)
    later_loads = load(momentum, mom, 2 * PIECES) + load(weights, wts, 3 * PIECES)
    for copy in tables + first_loads:
        copy.start()

    def peer(k):
        raised = me + k
        return jnp.where(raised >= n, raised - n, raised)

    barrier = pltpu.get_barrier_semaphore()

    def greet(k, _):
        pl.semaphore_signal(barrier, inc=1, device_id=(peer(k),), device_id_type=MESH)
        return 0

    lax.fori_loop(1, n, greet, 0)

    for copy in tables:
        copy.wait()
    my_row = me - band

    def flag_owner(o, _):
        used = cnt_s[my_row, o]
        listed = gcnt_s[o]
        picks = [jnp.where(c < used, sel_s[c, o], -1) for c in range(cap)]
        for j in range(list_len):
            block = ids[j, o]
            hit = picks[0] == block
            for pick in picks[1:]:
                hit = jnp.logical_or(hit, pick == block)
            hit = jnp.logical_and(hit, j < listed)
            flags[j, o] = jnp.where(hit, jnp.float32(1.0), jnp.float32(0.0))
        return 0

    lax.fori_loop(0, n, flag_owner, 0)

    for copy in first_loads:
        copy.wait()
    for copy in later_loads:
        copy.start()
    pl.semaphore_wait(barrier, n - 1)

    def pick_rows(o, target):
        for j in range(list_len):
            block = ids[j, o]
            row = acc[pl.ds(block, 1), :] + res_buf[pl.ds(block, 1), :]
            sent = row * flags[j, o]
            outgoing[o, pl.ds(j, 1), :] = sent
            if target is not None:
                target[o, pl.ds(j, 1), :] = sent
            kept[o, pl.ds(j, 1), :] = row - sent

    def send_to_owner(k, _):
        o = peer(k)
        pick_rows(o, None)
        pltpu.make_async_remote_copy(
            src_ref=outgoing.at[o], dst_ref=incoming.at[me],
            send_sem=send_sem, recv_sem=recv_sem,
            device_id=(o,), device_id_type=MESH,
        ).start()
        return 0

    lax.fori_loop(1, n, send_to_owner, 0)
    pick_rows(me, incoming)

    def all_of(buffer, send, recv):
        part = buffer.at[pl.ds(0, n - 1)]
        return pltpu.make_async_remote_copy(
            src_ref=part, dst_ref=part, send_sem=send, recv_sem=recv,
            device_id=(peer(1),), device_id_type=MESH,
        )

    for copy in later_loads:
        copy.wait()

    def pick_weights(o, _):
        for j in range(list_len):
            wrows[o, pl.ds(j, 1), :] = wts[pl.ds(ids[j, o], 1), :]
        return 0

    lax.fori_loop(0, n, pick_weights, 0)

    def dense_step(i, _):
        rows = pl.ds(pl.multiple_of(i * chunk, chunk), chunk)
        decayed = momentum_coef * mom[rows, :]
        mom[rows, :] = decayed
        wts[rows, :] = wts[rows, :] - learning_rate * decayed
        return 0

    lax.fori_loop(0, block_count // chunk, dense_step, 0)

    all_of(incoming, send_sem, recv_sem).wait_recv()
    updates[me] = jnp.sum(incoming[...], axis=0)

    def send_sum(k, _):
        pltpu.make_async_remote_copy(
            src_ref=updates.at[me], dst_ref=updates.at[me],
            send_sem=send2_sem, recv_sem=recv2_sem,
            device_id=(peer(k),), device_id_type=MESH,
        ).start()
        return 0

    lax.fori_loop(1, n, send_sum, 0)

    def dense_acc(i, _):
        rows = pl.ds(pl.multiple_of(i * chunk, chunk), chunk)
        acc[rows, :] = acc[rows, :] + res_buf[rows, :]
        return 0

    lax.fori_loop(0, block_count // chunk, dense_acc, 0)

    def pick_momentum(o, _):
        for j in range(list_len):
            mrows[o, pl.ds(j, 1), :] = mom[pl.ds(ids[j, o], 1), :]
        return 0

    lax.fori_loop(0, n, pick_momentum, 0)

    all_of(outgoing, send_sem, recv_sem).wait_send()
    all_of(updates, send2_sem, recv2_sem).wait_recv()
    new_rows = mrows[...] + updates[...]
    mrows[...] = new_rows
    wrows[...] = wrows[...] - learning_rate * new_rows
    all_of(updates, send2_sem, recv2_sem).wait_send()


def finish(
    ids, acc_in, mom_in, wts_in, kept, mrows, wrows,
    new_weights, new_momentum, new_residual, acc, mom, wts,
    sems,
):
    n, list_len = kept.shape[0], kept.shape[1]
    copies = []

    def place(*pairs):
        def step(o, _):
            for j in range(list_len):
                target = pl.ds(ids[j, o], 1)
                for rows, whole in pairs:
                    whole[target, :] = rows[o, pl.ds(j, 1), :]
            return 0

        lax.fori_loop(0, n, step, 0)

    def write(whole, result):
        copies.extend(pieces(whole, result, sems, len(copies)))
        for copy in copies[-PIECES:]:
            copy.start()

    place((kept, acc))
    write(acc, new_residual)
    place((mrows, mom), (wrows, wts))
    write(mom, new_momentum)
    write(wts, new_weights)
    for copy in copies:
        copy.wait()


def local(n, gradient, residual, weights, momentum, sel_idx, sel_count, gath_idx, gath_count):
    block_count, block_len = weights.shape
    cap, list_len = sel_idx.shape[2], gath_idx.shape[1]
    f32, i32 = jnp.float32, jnp.int32
    dense = pltpu.VMEM((block_count, block_len), f32)
    tiles = pltpu.VMEM((n, list_len, block_len), f32)
    table = pltpu.SMEM((list_len, n), i32)
    hbm = pl.BlockSpec(memory_space=pltpu.HBM)
    vmem = pl.BlockSpec(memory_space=pltpu.VMEM)
    smem = pl.BlockSpec(memory_space=pltpu.SMEM)
    dense_bytes = block_count * block_len * 4
    tile_bytes = n * list_len * block_len * 4
    chunk = 64

    acc, mom, wts, kept, mrows, wrows, ids = pl.pallas_call(
        functools.partial(exchange, n, chunk),
        out_shape=(dense, dense, dense, tiles, tiles, tiles, table),
        in_specs=[hbm] * 8,
        out_specs=[vmem] * 6 + [smem],
        scratch_shapes=[
            dense,
            pltpu.SMEM((cap, n), i32),
            pltpu.SMEM((ROWS, n), i32),
            pltpu.SMEM((n,), i32),
            pltpu.SMEM((list_len, n), f32),
            tiles,
            tiles,
            tiles,
            pltpu.SemaphoreType.DMA((4 * PIECES,)),
            pltpu.SemaphoreType.DMA((4,)),
            pltpu.SemaphoreType.DMA,
            pltpu.SemaphoreType.DMA,
            pltpu.SemaphoreType.DMA,
            pltpu.SemaphoreType.DMA,
        ],
        compiler_params=pltpu.CompilerParams(
            collective_id=0, has_side_effects=True,
            vmem_limit_bytes=dense_bytes + 4 * tile_bytes + (1 << 21),
        ),
        cost_estimate=pl.CostEstimate(
            flops=5 * block_count * block_len, bytes_accessed=4 * dense_bytes, transcendentals=0
        ),
        name="exchange",
    )(*[
        pltpu.with_memory_space_constraint(operand, pltpu.HBM)
        for operand in (
            gradient.reshape(block_count, block_len),
            residual.reshape(block_count, block_len),
            weights,
            momentum,
            sel_idx.transpose(0, 2, 1),
            sel_count,
            gath_idx.T,
            gath_count,
        )
    ])
    whole = jax.ShapeDtypeStruct((block_count, block_len), f32)
    new_weights, new_momentum, new_residual, _, _, _ = pl.pallas_call(
        finish,
        out_shape=(whole, whole, whole, dense, dense, dense),
        in_specs=[smem] + [vmem] * 6,
        out_specs=[hbm] * 3 + [vmem] * 3,
        input_output_aliases={1: 3, 2: 4, 3: 5},
        scratch_shapes=[pltpu.SemaphoreType.DMA((3 * PIECES,))],
        compiler_params=pltpu.CompilerParams(vmem_limit_bytes=1 << 21),
        cost_estimate=pl.CostEstimate(flops=0, bytes_accessed=3 * dense_bytes, transcendentals=0),
        name="finish",
    )(ids, acc, mom, wts, kept, mrows, wrows)
    return new_weights, new_momentum, new_residual[None]


def solution(mesh):
    placed = (P("dp", None, None), P("dp", None, None), P(), P(), P(), P(), P(), P())
    return jax.shard_map(
        functools.partial(local, mesh.shape["dp"]),
        mesh=mesh,
        in_specs=placed,
        out_specs=(P(), P(), P("dp", None, None)),
        check_vma=False,
    )
```

```python
import functools

import jax
import jax.numpy as jnp
from jax import lax
from jax.experimental import pallas as pl
from jax.experimental.pallas import tpu as pltpu
from jax.sharding import PartitionSpec as P

MESH = pl.DeviceIdType.MESH
momentum_coef = 0.9
learning_rate = 0.05
ROWS = 8
PIECES = 2


def pieces(source, target, sems, first):
    rows = source.shape[0] // PIECES
    return [
        pltpu.make_async_copy(
            source.at[pl.ds(i * rows, rows)], target.at[pl.ds(i * rows, rows)], sems.at[first + i]
        )
        for i in range(PIECES)
    ]


def exchange(
    n, chunk,
    grad, resid, weights, momentum, sel, counts, lists, list_counts,
    acc, mom, wts, kept, mrows, wrows, ids,
    res_buf, sel_s, cnt_s, gcnt_s, flags, outgoing, beside, incoming, updates,
    load_sem, table_sem, send_sems, recv_sems,
):
    half = n // 2
    me = lax.axis_index("dp")
    chip, core = me // 2, me % 2
    other = 1 - core
    sibling = 2 * chip + other
    cap, list_len = sel_s.shape[0], ids.shape[0]
    block_count = acc.shape[0]
    mine, theirs = core * half, other * half

    def chip_at(k):
        raised = chip + k
        return jnp.where(raised >= half, raised - half, raised)

    band = pl.multiple_of((me // ROWS) * ROWS, ROWS)
    tables = [
        pltpu.make_async_copy(lists, ids, table_sem.at[0]),
        pltpu.make_async_copy(sel.at[me], sel_s, table_sem.at[1]),
        pltpu.make_async_copy(counts.at[pl.ds(band, ROWS)], cnt_s, table_sem.at[2]),
        pltpu.make_async_copy(list_counts, gcnt_s, table_sem.at[3]),
    ]

    def load(source, target, first):
        return pieces(source, target, load_sem, first)

    first_loads = load(grad, acc, 0) + load(resid, res_buf, PIECES)
    later_loads = load(momentum, mom, 2 * PIECES) + load(weights, wts, 3 * PIECES)
    for copy in tables + first_loads:
        copy.start()

    barrier = pltpu.get_barrier_semaphore()

    def greet(k, _):
        pl.semaphore_signal(
            barrier, inc=1, device_id=(2 * chip_at(k) + core,), device_id_type=MESH
        )
        return 0

    lax.fori_loop(1, half, greet, 0)
    pl.semaphore_signal(barrier, inc=1, device_id=(sibling,), device_id_type=MESH)

    for copy in tables:
        copy.wait()
    my_row = me - band

    def flag_owner(o, _):
        used = cnt_s[my_row, o]
        listed = gcnt_s[o]
        picks = [jnp.where(c < used, sel_s[c, o], -1) for c in range(cap)]
        for j in range(list_len):
            block = ids[j, o]
            hit = picks[0] == block
            for pick in picks[1:]:
                hit = jnp.logical_or(hit, pick == block)
            hit = jnp.logical_and(hit, j < listed)
            flags[j, o] = jnp.where(hit, jnp.float32(1.0), jnp.float32(0.0))
        return 0

    lax.fori_loop(0, n, flag_owner, 0)

    for copy in first_loads:
        copy.wait()
    for copy in later_loads:
        copy.start()

    def pick_for(side):
        def pick_rows(c, _):
            o, slot = 2 * c + side, side * half + c
            for j in range(list_len):
                block = ids[j, o]
                row = acc[pl.ds(block, 1), :] + res_buf[pl.ds(block, 1), :]
                sent = row * flags[j, o]
                outgoing[slot, pl.ds(j, 1), :] = sent
                kept[slot, pl.ds(j, 1), :] = row - sent
            return 0

        lax.fori_loop(0, half, pick_rows, 0)

    def remote(source, target, phase, device):
        return pltpu.make_async_remote_copy(
            src_ref=source, dst_ref=target,
            send_sem=send_sems.at[phase], recv_sem=recv_sems.at[phase],
            device_id=(device,), device_id_type=MESH,
        )

    pick_for(other)
    pl.semaphore_wait(barrier, half)
    swap = remote(outgoing.at[pl.ds(theirs, half)], beside, 0, sibling)
    swap.start()
    pick_for(core)
    swap.wait_recv()

    def send_to_owner(k, _):
        c = chip_at(k)
        outgoing[mine + c] = outgoing[mine + c] + beside[c]
        remote(outgoing.at[mine + c], incoming.at[chip], 1, 2 * c + core).start()
        return 0

    lax.fori_loop(1, half, send_to_owner, 0)
    incoming[chip] = outgoing[mine + chip] + beside[chip]

    def all_peers(phase):
        part = incoming.at[pl.ds(0, half - 1)]
        return remote(part, part, phase, sibling)

    def dense_acc(i, _):
        rows = pl.ds(pl.multiple_of(i * chunk, chunk), chunk)
        acc[rows, :] = acc[rows, :] + res_buf[rows, :]
        return 0

    lax.fori_loop(0, block_count // chunk, dense_acc, 0)
    all_peers(1).wait_recv()
    updates[mine + chip] = jnp.sum(incoming[...], axis=0)

    def send_sum(k, _):
        own = updates.at[mine + chip]
        remote(own, own, 2, 2 * chip_at(k) + core).start()
        return 0

    lax.fori_loop(1, half, send_sum, 0)

    for copy in later_loads:
        copy.wait()

    def pick_weights(c, _):
        for side in range(2):
            for j in range(list_len):
                block = pl.ds(ids[j, 2 * c + side], 1)
                wrows[side * half + c, pl.ds(j, 1), :] = wts[block, :]
                mrows[side * half + c, pl.ds(j, 1), :] = mom[block, :]
        return 0

    lax.fori_loop(0, half, pick_weights, 0)

    def dense_step(i, _):
        rows = pl.ds(pl.multiple_of(i * chunk, chunk), chunk)
        decayed = momentum_coef * mom[rows, :]
        mom[rows, :] = decayed
        wts[rows, :] = wts[rows, :] - learning_rate * decayed
        return 0

    lax.fori_loop(0, block_count // chunk, dense_step, 0)

    def apply_sums(first):
        part = pl.ds(first, half)
        new_rows = momentum_coef * mrows[part] + updates[part]
        mrows[part] = new_rows
        wrows[part] = wrows[part] - learning_rate * new_rows

    all_peers(2).wait_recv()
    own_side = updates.at[pl.ds(mine, half)]
    relay = remote(own_side, own_side, 3, sibling)
    relay.start()
    apply_sums(mine)
    swap.wait_send()
    all_peers(1).wait_send()
    all_peers(2).wait_send()
    relay.wait_recv()
    apply_sums(theirs)
    relay.wait_send()


def finish(
    ids, acc_in, mom_in, wts_in, kept, mrows, wrows,
    new_weights, new_momentum, new_residual, acc, mom, wts,
    sems,
):
    half, list_len = kept.shape[0] // 2, kept.shape[1]
    copies = []

    def place(*pairs):
        def step(c, _):
            for side in range(2):
                for j in range(list_len):
                    target = pl.ds(ids[j, 2 * c + side], 1)
                    for rows, whole in pairs:
                        whole[target, :] = rows[side * half + c, pl.ds(j, 1), :]
            return 0

        lax.fori_loop(0, half, step, 0)

    def write(whole, result):
        copies.extend(pieces(whole, result, sems, len(copies)))
        for copy in copies[-PIECES:]:
            copy.start()

    place((kept, acc))
    write(acc, new_residual)
    place((mrows, mom), (wrows, wts))
    write(mom, new_momentum)
    write(wts, new_weights)
    for copy in copies:
        copy.wait()


def local(n, gradient, residual, weights, momentum, sel_idx, sel_count, gath_idx, gath_count):
    block_count, block_len = weights.shape
    cap, list_len = sel_idx.shape[2], gath_idx.shape[1]
    f32, i32 = jnp.float32, jnp.int32
    dense = pltpu.VMEM((block_count, block_len), f32)
    tiles = pltpu.VMEM((n, list_len, block_len), f32)
    half_tiles = pltpu.VMEM((n // 2, list_len, block_len), f32)
    table = pltpu.SMEM((list_len, n), i32)
    hbm = pl.BlockSpec(memory_space=pltpu.HBM)
    vmem = pl.BlockSpec(memory_space=pltpu.VMEM)
    smem = pl.BlockSpec(memory_space=pltpu.SMEM)
    dense_bytes = block_count * block_len * 4
    tile_bytes = n * list_len * block_len * 4
    chunk = 64

    acc, mom, wts, kept, mrows, wrows, ids = pl.pallas_call(
        functools.partial(exchange, n, chunk),
        out_shape=(dense, dense, dense, tiles, tiles, tiles, table),
        in_specs=[hbm] * 8,
        out_specs=[vmem] * 6 + [smem],
        scratch_shapes=[
            dense,
            pltpu.SMEM((cap, n), i32),
            pltpu.SMEM((ROWS, n), i32),
            pltpu.SMEM((n,), i32),
            pltpu.SMEM((list_len, n), f32),
            tiles,
            half_tiles,
            half_tiles,
            tiles,
            pltpu.SemaphoreType.DMA((4 * PIECES,)),
            pltpu.SemaphoreType.DMA((4,)),
            pltpu.SemaphoreType.DMA((4,)),
            pltpu.SemaphoreType.DMA((4,)),
        ],
        compiler_params=pltpu.CompilerParams(
            collective_id=0, has_side_effects=True,
            vmem_limit_bytes=dense_bytes + 4 * tile_bytes + (1 << 21),
        ),
        cost_estimate=pl.CostEstimate(
            flops=5 * block_count * block_len, bytes_accessed=4 * dense_bytes, transcendentals=0
        ),
        name="exchange",
    )(*[
        pltpu.with_memory_space_constraint(operand, pltpu.HBM)
        for operand in (
            gradient.reshape(block_count, block_len),
            residual.reshape(block_count, block_len),
            weights,
            momentum,
            sel_idx.transpose(0, 2, 1),
            sel_count,
            gath_idx.T,
            gath_count,
        )
    ])
    whole = jax.ShapeDtypeStruct((block_count, block_len), f32)
    new_weights, new_momentum, new_residual, _, _, _ = pl.pallas_call(
        finish,
        out_shape=(whole, whole, whole, dense, dense, dense),
        in_specs=[smem] + [vmem] * 6,
        out_specs=[hbm] * 3 + [vmem] * 3,
        input_output_aliases={1: 3, 2: 4, 3: 5},
        scratch_shapes=[pltpu.SemaphoreType.DMA((3 * PIECES,))],
        compiler_params=pltpu.CompilerParams(vmem_limit_bytes=1 << 21),
        cost_estimate=pl.CostEstimate(flops=0, bytes_accessed=3 * dense_bytes, transcendentals=0),
        name="finish",
    )(ids, acc, mom, wts, kept, mrows, wrows)
    return new_weights, new_momentum, new_residual[None]


def solution(mesh):
    placed = (P("dp", None, None), P("dp", None, None), P(), P(), P(), P(), P(), P())
    return jax.shard_map(
        functools.partial(local, mesh.shape["dp"]),
        mesh=mesh,
        in_specs=placed,
        out_specs=(P(), P(), P("dp", None, None)),
        check_vma=False,
    )
```

```python
import functools

import jax
import jax.numpy as jnp
from jax import lax
from jax.experimental import pallas as pl
from jax.experimental.pallas import tpu as pltpu
from jax.sharding import PartitionSpec as P

MESH = pl.DeviceIdType.MESH
momentum_coef = 0.9
learning_rate = 0.05
ROWS = 8
PIECES = 2


def pieces(source, target, sems, first):
    rows = source.shape[0] // PIECES
    return [
        pltpu.make_async_copy(
            source.at[pl.ds(i * rows, rows)], target.at[pl.ds(i * rows, rows)], sems.at[first + i]
        )
        for i in range(PIECES)
    ]


def exchange(
    n, chunk,
    grad, resid, weights, momentum, sel, counts, lists, list_counts,
    acc, mom, wts, kept, mrows, wrows, ids,
    res_buf, sel_v, cnt_v, gcnt_v, ids_v, flags_v, flags, outgoing, beside, incoming, updates,
    load_sem, table_sem, send_sems, recv_sems,
):
    half = n // 2
    me = lax.axis_index("dp")
    chip, core = me // 2, me % 2
    other = 1 - core
    sibling = 2 * chip + other
    cap, list_len = sel_v.shape[0], ids.shape[0]
    block_count = acc.shape[0]
    mine, theirs = core * half, other * half

    def chip_at(k):
        raised = chip + k
        return jnp.where(raised >= half, raised - half, raised)

    band = pl.multiple_of((me // ROWS) * ROWS, ROWS)
    tables = [
        pltpu.make_async_copy(lists, ids, table_sem.at[0]),
        pltpu.make_async_copy(sel.at[me], sel_v, table_sem.at[1]),
        pltpu.make_async_copy(counts.at[pl.ds(band, ROWS)], cnt_v, table_sem.at[2]),
        pltpu.make_async_copy(list_counts, gcnt_v, table_sem.at[3]),
        pltpu.make_async_copy(lists, ids_v, table_sem.at[4]),
    ]

    def load(source, target, first):
        return pieces(source, target, load_sem, first)

    first_loads = load(grad, acc, 0) + load(resid, res_buf, PIECES)
    later_loads = load(momentum, mom, 2 * PIECES) + load(weights, wts, 3 * PIECES)
    for copy in tables + first_loads:
        copy.start()

    barrier = pltpu.get_barrier_semaphore()

    def greet(k, _):
        pl.semaphore_signal(
            barrier, inc=1, device_id=(2 * chip_at(k) + core,), device_id_type=MESH
        )
        return 0

    lax.fori_loop(1, half, greet, 0)
    pl.semaphore_signal(barrier, inc=1, device_id=(sibling,), device_id_type=MESH)

    for copy in tables:
        copy.wait()
    used = cnt_v[pl.ds(me - band, 1), :]
    listed = gcnt_v[...].reshape(1, n)
    blocks = ids_v[...]
    hit = jnp.zeros((list_len, n), jnp.float32)
    for c in range(cap):
        picked = jnp.where(c < used, sel_v[pl.ds(c, 1), :], -1)
        hit = jnp.where(blocks == picked, 1.0, hit)
    slots = lax.broadcasted_iota(jnp.int32, (list_len, n), 0)
    flags_v[...] = jnp.where(slots < listed, hit, 0.0)
    flag_copy = pltpu.make_async_copy(flags_v, flags, table_sem.at[0])
    flag_copy.start()

    for copy in first_loads:
        copy.wait()
    for copy in later_loads:
        copy.start()
    flag_copy.wait()

    def pick_for(side):
        def pick_rows(c, _):
            o, slot = 2 * c + side, side * half + c
            rows = [pl.ds(ids[j, o], 1) for j in range(list_len)]
            rows = [acc[row, :] + res_buf[row, :] for row in rows]
            sent = [row * flags[j, o] for j, row in enumerate(rows)]
            for j in range(list_len):
                outgoing[slot, pl.ds(j, 1), :] = sent[j]
                kept[slot, pl.ds(j, 1), :] = rows[j] - sent[j]
            return 0

        lax.fori_loop(0, half, pick_rows, 0)

    def remote(source, target, phase, device):
        return pltpu.make_async_remote_copy(
            src_ref=source, dst_ref=target,
            send_sem=send_sems.at[phase], recv_sem=recv_sems.at[phase],
            device_id=(device,), device_id_type=MESH,
        )

    pick_for(other)
    pl.semaphore_wait(barrier, half)
    swap = remote(outgoing.at[pl.ds(theirs, half)], beside, 0, sibling)
    swap.start()
    pick_for(core)
    swap.wait_recv()

    def send_to_owner(k, _):
        c = chip_at(k)
        outgoing[mine + c] = outgoing[mine + c] + beside[c]
        remote(outgoing.at[mine + c], incoming.at[chip], 1, 2 * c + core).start()
        return 0

    lax.fori_loop(1, half, send_to_owner, 0)
    incoming[chip] = outgoing[mine + chip] + beside[chip]

    def all_peers(phase):
        part = incoming.at[pl.ds(0, half - 1)]
        return remote(part, part, phase, sibling)

    def dense_acc(i, _):
        rows = pl.ds(pl.multiple_of(i * chunk, chunk), chunk)
        acc[rows, :] = acc[rows, :] + res_buf[rows, :]
        return 0

    lax.fori_loop(0, block_count // chunk, dense_acc, 0)
    all_peers(1).wait_recv()
    updates[mine + chip] = jnp.sum(incoming[...], axis=0)

    def send_sum(k, _):
        own = updates.at[mine + chip]
        remote(own, own, 2, 2 * chip_at(k) + core).start()
        return 0

    lax.fori_loop(1, half, send_sum, 0)

    for copy in later_loads:
        copy.wait()

    def pick_weights(c, _):
        places = [(side, j) for side in range(2) for j in range(list_len)]
        blocks = [pl.ds(ids[j, 2 * c + side], 1) for side, j in places]
        found = [(wts[block, :], mom[block, :]) for block in blocks]
        for (side, j), (weight, moment) in zip(places, found):
            wrows[side * half + c, pl.ds(j, 1), :] = weight
            mrows[side * half + c, pl.ds(j, 1), :] = moment
        return 0

    lax.fori_loop(0, half, pick_weights, 0)

    def dense_step(i, _):
        rows = pl.ds(pl.multiple_of(i * chunk, chunk), chunk)
        decayed = momentum_coef * mom[rows, :]
        mom[rows, :] = decayed
        wts[rows, :] = wts[rows, :] - learning_rate * decayed
        return 0

    lax.fori_loop(0, block_count // chunk, dense_step, 0)

    def apply_sums(first):
        part = pl.ds(first, half)
        new_rows = momentum_coef * mrows[part] + updates[part]
        mrows[part] = new_rows
        wrows[part] = wrows[part] - learning_rate * new_rows

    all_peers(2).wait_recv()
    own_side = updates.at[pl.ds(mine, half)]
    relay = remote(own_side, own_side, 3, sibling)
    relay.start()
    apply_sums(mine)
    swap.wait_send()
    all_peers(1).wait_send()
    all_peers(2).wait_send()
    relay.wait_recv()
    apply_sums(theirs)
    relay.wait_send()


def finish(
    ids, acc_in, mom_in, wts_in, kept, mrows, wrows,
    new_weights, new_momentum, new_residual, acc, mom, wts,
    sems,
):
    half, list_len = kept.shape[0] // 2, kept.shape[1]
    copies = []

    def place(*pairs):
        def step(c, _):
            places = [(side, j) for side in range(2) for j in range(list_len)]
            targets = [pl.ds(ids[j, 2 * c + side], 1) for side, j in places]
            for rows, whole in pairs:
                values = [rows[side * half + c, pl.ds(j, 1), :] for side, j in places]
                for target, value in zip(targets, values):
                    whole[target, :] = value
            return 0

        lax.fori_loop(0, half, step, 0)

    def write(whole, result):
        copies.extend(pieces(whole, result, sems, len(copies)))
        for copy in copies[-PIECES:]:
            copy.start()

    place((kept, acc))
    write(acc, new_residual)
    place((mrows, mom), (wrows, wts))
    write(mom, new_momentum)
    write(wts, new_weights)
    for copy in copies:
        copy.wait()


def local(n, gradient, residual, weights, momentum, sel_idx, sel_count, gath_idx, gath_count):
    block_count, block_len = weights.shape
    cap, list_len = sel_idx.shape[2], gath_idx.shape[1]
    f32, i32 = jnp.float32, jnp.int32
    dense = pltpu.VMEM((block_count, block_len), f32)
    tiles = pltpu.VMEM((n, list_len, block_len), f32)
    half_tiles = pltpu.VMEM((n // 2, list_len, block_len), f32)
    table = pltpu.SMEM((list_len, n), i32)
    hbm = pl.BlockSpec(memory_space=pltpu.HBM)
    vmem = pl.BlockSpec(memory_space=pltpu.VMEM)
    smem = pl.BlockSpec(memory_space=pltpu.SMEM)
    dense_bytes = block_count * block_len * 4
    tile_bytes = n * list_len * block_len * 4
    chunk = 256

    acc, mom, wts, kept, mrows, wrows, ids = pl.pallas_call(
        functools.partial(exchange, n, chunk),
        out_shape=(dense, dense, dense, tiles, tiles, tiles, table),
        in_specs=[hbm] * 8,
        out_specs=[vmem] * 6 + [smem],
        scratch_shapes=[
            dense,
            pltpu.VMEM((cap, n), i32),
            pltpu.VMEM((ROWS, n), i32),
            pltpu.VMEM((n,), i32),
            pltpu.VMEM((list_len, n), i32),
            pltpu.VMEM((list_len, n), f32),
            pltpu.SMEM((list_len, n), f32),
            tiles,
            half_tiles,
            half_tiles,
            tiles,
            pltpu.SemaphoreType.DMA((4 * PIECES,)),
            pltpu.SemaphoreType.DMA((5,)),
            pltpu.SemaphoreType.DMA((4,)),
            pltpu.SemaphoreType.DMA((4,)),
        ],
        compiler_params=pltpu.CompilerParams(
            collective_id=0, has_side_effects=True,
            vmem_limit_bytes=dense_bytes + 4 * tile_bytes + (1 << 21),
        ),
        cost_estimate=pl.CostEstimate(
            flops=5 * block_count * block_len, bytes_accessed=4 * dense_bytes, transcendentals=0
        ),
        name="exchange",
    )(*[
        pltpu.with_memory_space_constraint(operand, pltpu.HBM)
        for operand in (
            gradient.reshape(block_count, block_len),
            residual.reshape(block_count, block_len),
            weights,
            momentum,
            sel_idx.transpose(0, 2, 1),
            sel_count,
            gath_idx.T,
            gath_count,
        )
    ])
    whole = jax.ShapeDtypeStruct((block_count, block_len), f32)
    new_weights, new_momentum, new_residual, _, _, _ = pl.pallas_call(
        finish,
        out_shape=(whole, whole, whole, dense, dense, dense),
        in_specs=[smem] + [vmem] * 6,
        out_specs=[hbm] * 3 + [vmem] * 3,
        input_output_aliases={1: 3, 2: 4, 3: 5},
        scratch_shapes=[pltpu.SemaphoreType.DMA((3 * PIECES,))],
        compiler_params=pltpu.CompilerParams(vmem_limit_bytes=1 << 21),
        cost_estimate=pl.CostEstimate(flops=0, bytes_accessed=3 * dense_bytes, transcendentals=0),
        name="finish",
    )(ids, acc, mom, wts, kept, mrows, wrows)
    return new_weights, new_momentum, new_residual[None]


def solution(mesh):
    placed = (P("dp", None, None), P("dp", None, None), P(), P(), P(), P(), P(), P())
    return jax.shard_map(
        functools.partial(local, mesh.shape["dp"]),
        mesh=mesh,
        in_specs=placed,
        out_specs=(P(), P(), P("dp", None, None)),
        check_vma=False,
    )
```

```python
import functools

import jax
import jax.numpy as jnp
from jax import lax
from jax.experimental import pallas as pl
from jax.experimental.pallas import tpu as pltpu
from jax.sharding import PartitionSpec as P

MESH = pl.DeviceIdType.MESH
momentum_coef = 0.9
learning_rate = 0.05
ROWS = 8
PIECES = 2


def pieces(source, target, sems, first):
    rows = source.shape[0] // PIECES
    return [
        pltpu.make_async_copy(
            source.at[pl.ds(i * rows, rows)], target.at[pl.ds(i * rows, rows)], sems.at[first + i]
        )
        for i in range(PIECES)
    ]


def exchange(
    n, chunk,
    grad, resid, weights, momentum, sel, counts, lists, list_counts,
    acc, mom, wts, kept, mrows, wrows, ids,
    res_buf, sel_s, cnt_s, gcnt_s, flags, sel_v, cnt_v, gcnt_v, ids_v, flags_v,
    outgoing, incoming, sender_blocks, updates,
    load_sem, table_sem, send_sems, recv_sems,
):
    me = lax.axis_index("dp")
    cap, list_len = sel_s.shape[0], ids.shape[0]
    block_count, block_len = acc.shape

    band = pl.multiple_of((me // ROWS) * ROWS, ROWS)
    tables = [
        pltpu.make_async_copy(source, target, table_sem.at[i])
        for i, (source, target) in enumerate((
            (lists, ids), (sel.at[me], sel_s), (counts.at[pl.ds(band, ROWS)], cnt_s), (list_counts, gcnt_s),
            (sel, sel_v), (counts.at[pl.ds(band, ROWS)], cnt_v), (list_counts, gcnt_v), (lists, ids_v),
        ))
    ]

    def load(source, target, first):
        return pieces(source, target, load_sem, first)

    first_loads = load(grad, acc, 0) + load(resid, res_buf, PIECES)
    later_loads = load(momentum, mom, 2 * PIECES) + load(weights, wts, 3 * PIECES)
    for copy in tables[:4] + first_loads + tables[4:]:
        copy.start()

    bits = [1 << i for i in range((n - 1).bit_length())]
    my_bits = [(me // bit) % 2 for bit in bits]

    def peer(step):
        k = n - step
        both = sum(mine * ((k // bit) % 2) * bit for mine, bit in zip(my_bits, bits))
        return me + k - 2 * both

    barrier = pltpu.get_barrier_semaphore()

    def greet(step, _):
        pl.semaphore_signal(barrier, inc=1, device_id=(peer(step),), device_id_type=MESH)
        return 0

    lax.fori_loop(1, n, greet, 0)

    for copy in tables:
        copy.wait()
    my_row = me - band
    used = cnt_v[pl.ds(my_row, 1), :]
    listed = gcnt_v[...].reshape(1, n)
    blocks = ids_v[...]
    selected = sel_v[me]
    hit = jnp.zeros((list_len, n), jnp.float32)
    for c in range(cap):
        picked = jnp.where(c < used, selected[c:c + 1, :], -1)
        hit = jnp.where(blocks == picked, 1.0, hit)
    slots = lax.broadcasted_iota(jnp.int32, (list_len, n), 0)
    flags_v[...] = jnp.where(slots < listed, hit, 0.0)
    flag_copy = pltpu.make_async_copy(flags_v, flags, table_sem.at[0])
    flag_copy.start()
    lanes = lax.broadcasted_iota(jnp.int32, (n, cap, n), 2)
    for_me = jnp.where(lanes == me, sel_v[...].astype(jnp.float32), 0.0)
    sender_blocks[...] = jnp.broadcast_to(
        jnp.sum(for_me, axis=2, keepdims=True), (n, cap, block_len)
    )

    for copy in first_loads:
        copy.wait()
    for copy in later_loads:
        copy.start()

    def pick_rows(o, _):
        rows = [pl.ds(sel_s[c, o], 1) for c in range(cap)]
        rows = [acc[row, :] + res_buf[row, :] for row in rows]
        count = cnt_s[my_row, o]
        for c in range(cap):
            outgoing[o, pl.ds(c, 1), :] = rows[c] * jnp.where(c < count, 1.0, 0.0)
        return 0

    lax.fori_loop(0, n, pick_rows, 0)

    def remote(source, target, phase, device):
        return pltpu.make_async_remote_copy(
            src_ref=source, dst_ref=target,
            send_sem=send_sems.at[phase], recv_sem=recv_sems.at[phase],
            device_id=(device,), device_id_type=MESH,
        )

    def all_peers(buffer, phase):
        part = buffer.at[pl.ds(0, n - 1)]
        return remote(part, part, phase, peer(1))

    pl.semaphore_wait(barrier, n - 1)

    def send_to_owner(step, _):
        o = peer(step)
        remote(outgoing.at[o], incoming.at[me], 0, o).start()
        return 0

    lax.fori_loop(1, n, send_to_owner, 0)
    incoming[me] = outgoing[me]

    def dense_acc(i, _):
        rows = pl.ds(pl.multiple_of(i * chunk, chunk), chunk)
        acc[rows, :] = acc[rows, :] + res_buf[rows, :]
        return 0

    lax.fori_loop(0, block_count // chunk, dense_acc, 0)
    my_count = gcnt_s[me]
    all_peers(incoming, 0).wait_recv()
    for j in range(list_len):
        block = jnp.where(j < my_count, ids[j, me], -1).astype(jnp.float32)
        chosen = jnp.where(sender_blocks[...] == block, incoming[...], 0.0)
        updates[me, pl.ds(j, 1), :] = jnp.sum(jnp.sum(chosen, axis=0), axis=0, keepdims=True)

    def send_sum(step, _):
        remote(updates.at[me], updates.at[me], 1, peer(step)).start()
        return 0

    lax.fori_loop(1, n, send_sum, 0)
    flag_copy.wait()

    def pick_kept(o, _):
        rows = [acc[pl.ds(ids[j, o], 1), :] for j in range(list_len)]
        for j in range(list_len):
            kept[o, pl.ds(j, 1), :] = rows[j] * (1.0 - flags[j, o])
        return 0

    lax.fori_loop(0, n, pick_kept, 0)
    for copy in later_loads:
        copy.wait()

    def pick_weights(o, _):
        blocks = [pl.ds(ids[j, o], 1) for j in range(list_len)]
        found = [(wts[block, :], mom[block, :]) for block in blocks]
        for j, (weight, moment) in enumerate(found):
            wrows[o, pl.ds(j, 1), :] = weight
            mrows[o, pl.ds(j, 1), :] = moment
        return 0

    lax.fori_loop(0, n, pick_weights, 0)

    def dense_step(i, _):
        rows = pl.ds(pl.multiple_of(i * chunk, chunk), chunk)
        decayed = momentum_coef * mom[rows, :]
        mom[rows, :] = decayed
        wts[rows, :] = wts[rows, :] - learning_rate * decayed
        return 0

    lax.fori_loop(0, block_count // chunk, dense_step, 0)
    all_peers(outgoing, 0).wait_send()
    all_peers(updates, 1).wait_recv()
    new_rows = momentum_coef * mrows[...] + updates[...]
    mrows[...] = new_rows
    wrows[...] = wrows[...] - learning_rate * new_rows
    all_peers(updates, 1).wait_send()


def finish(
    ids, acc_in, mom_in, wts_in, kept, mrows, wrows,
    new_weights, new_momentum, new_residual, acc, mom, wts,
    sems,
):
    half, list_len = kept.shape[0] // 2, kept.shape[1]
    copies = []

    def place(*pairs):
        def step(c, _):
            places = [(side, j) for side in range(2) for j in range(list_len)]
            targets = [pl.ds(ids[j, 2 * c + side], 1) for side, j in places]
            for rows, whole in pairs:
                values = [rows[2 * c + side, pl.ds(j, 1), :] for side, j in places]
                for target, value in zip(targets, values):
                    whole[target, :] = value
            return 0

        lax.fori_loop(0, half, step, 0)

    def write(whole, result):
        copies.extend(pieces(whole, result, sems, len(copies)))
        for copy in copies[-PIECES:]:
            copy.start()

    place((kept, acc))
    write(acc, new_residual)
    place((mrows, mom), (wrows, wts))
    write(mom, new_momentum)
    write(wts, new_weights)
    for copy in copies:
        copy.wait()


def local(n, gradient, residual, weights, momentum, sel_idx, sel_count, gath_idx, gath_count):
    block_count, block_len = weights.shape
    cap, list_len = sel_idx.shape[2], gath_idx.shape[1]
    f32, i32 = jnp.float32, jnp.int32
    dense = pltpu.VMEM((block_count, block_len), f32)
    tiles = pltpu.VMEM((n, list_len, block_len), f32)
    picks = pltpu.VMEM((n, cap, block_len), f32)
    table = pltpu.SMEM((list_len, n), i32)
    hbm = pl.BlockSpec(memory_space=pltpu.HBM)
    vmem = pl.BlockSpec(memory_space=pltpu.VMEM)
    smem = pl.BlockSpec(memory_space=pltpu.SMEM)
    dense_bytes = block_count * block_len * 4
    tile_bytes = n * list_len * block_len * 4
    chunk = 256

    acc, mom, wts, kept, mrows, wrows, ids = pl.pallas_call(
        functools.partial(exchange, n, chunk),
        out_shape=(dense, dense, dense, tiles, tiles, tiles, table),
        in_specs=[hbm] * 8,
        out_specs=[vmem] * 6 + [smem],
        scratch_shapes=[
            dense,
            pltpu.SMEM((cap, n), i32),
            pltpu.SMEM((ROWS, n), i32),
            pltpu.SMEM((n,), i32),
            pltpu.SMEM((list_len, n), f32),
            pltpu.VMEM((n, cap, n), i32),
            pltpu.VMEM((ROWS, n), i32),
            pltpu.VMEM((n,), i32),
            pltpu.VMEM((list_len, n), i32),
            pltpu.VMEM((list_len, n), f32),
            picks,
            picks,
            picks,
            tiles,
            pltpu.SemaphoreType.DMA((4 * PIECES,)),
            pltpu.SemaphoreType.DMA((8,)),
            pltpu.SemaphoreType.DMA((2,)),
            pltpu.SemaphoreType.DMA((2,)),
        ],
        compiler_params=pltpu.CompilerParams(
            collective_id=0, has_side_effects=True,
            vmem_limit_bytes=dense_bytes + 8 * tile_bytes + (1 << 21),
        ),
        cost_estimate=pl.CostEstimate(
            flops=5 * block_count * block_len, bytes_accessed=4 * dense_bytes, transcendentals=0
        ),
        name="exchange",
    )(*[
        pltpu.with_memory_space_constraint(operand, pltpu.HBM)
        for operand in (
            gradient.reshape(block_count, block_len),
            residual.reshape(block_count, block_len),
            weights,
            momentum,
            sel_idx.transpose(0, 2, 1),
            sel_count,
            gath_idx.T,
            gath_count,
        )
    ])
    whole = jax.ShapeDtypeStruct((block_count, block_len), f32)
    new_weights, new_momentum, new_residual, _, _, _ = pl.pallas_call(
        finish,
        out_shape=(whole, whole, whole, dense, dense, dense),
        in_specs=[smem] + [vmem] * 6,
        out_specs=[hbm] * 3 + [vmem] * 3,
        input_output_aliases={1: 3, 2: 4, 3: 5},
        scratch_shapes=[pltpu.SemaphoreType.DMA((3 * PIECES,))],
        compiler_params=pltpu.CompilerParams(vmem_limit_bytes=1 << 21),
        cost_estimate=pl.CostEstimate(flops=0, bytes_accessed=3 * dense_bytes, transcendentals=0),
        name="finish",
    )(ids, acc, mom, wts, kept, mrows, wrows)
    return new_weights, new_momentum, new_residual[None]


def solution(mesh):
    placed = (P("dp", None, None), P("dp", None, None), P(), P(), P(), P(), P(), P())
    return jax.shard_map(
        functools.partial(local, mesh.shape["dp"]),
        mesh=mesh,
        in_specs=placed,
        out_specs=(P(), P(), P("dp", None, None)),
        check_vma=False,
    )
```

```python
import functools

import jax
import jax.numpy as jnp
from jax import lax
from jax.experimental import pallas as pl
from jax.experimental.pallas import tpu as pltpu
from jax.sharding import PartitionSpec as P

MESH = pl.DeviceIdType.MESH
momentum_coef = 0.9
learning_rate = 0.05
ROWS = 8
PIECES = 2


def pieces(source, target, sems, first):
    rows = source.shape[0] // PIECES
    return [
        pltpu.make_async_copy(
            source.at[pl.ds(i * rows, rows)], target.at[pl.ds(i * rows, rows)], sems.at[first + i]
        )
        for i in range(PIECES)
    ]


def exchange(
    n, chunk,
    grad, resid, weights, momentum, sel, counts, lists, list_counts,
    acc, mom, wts, kept, mrows, wrows, ids,
    res_buf, sel_s, cnt_s, gcnt_s, flags, sel_v, cnt_v, gcnt_v, ids_v, flags_v,
    outgoing, incoming, sender_blocks, updates,
    load_sem, table_sem, send_sems, recv_sems,
):
    half = n // 2
    me = lax.axis_index("dp")
    cap, list_len = sel_s.shape[0], ids.shape[0]
    block_count, block_len = acc.shape

    band = pl.multiple_of((me // ROWS) * ROWS, ROWS)
    tables = [
        pltpu.make_async_copy(source, target, table_sem.at[i])
        for i, (source, target) in enumerate((
            (lists, ids), (sel.at[me], sel_s), (counts.at[pl.ds(band, ROWS)], cnt_s), (list_counts, gcnt_s),
            (sel, sel_v), (counts.at[pl.ds(band, ROWS)], cnt_v), (list_counts, gcnt_v), (lists, ids_v),
        ))
    ]

    def load(source, target, first):
        return pieces(source, target, load_sem, first)

    first_loads = load(grad, acc, 0) + load(resid, res_buf, PIECES)
    later_loads = load(momentum, mom, 2 * PIECES) + load(weights, wts, 3 * PIECES)
    for copy in tables[:4] + first_loads + tables[4:]:
        copy.start()

    owner = me < half
    share = 2 * me

    def each_other(stop, act):
        def step(device, _):
            @pl.when(device != me)
            def _():
                act(device)
            return 0

        lax.fori_loop(0, stop, step, 0)

    barrier = pltpu.get_barrier_semaphore()

    def greet(device):
        pl.semaphore_signal(barrier, inc=1, device_id=(device,), device_id_type=MESH)

    each_other(half, greet)

    @pl.when(owner)
    def _():
        lax.fori_loop(half, n, lambda device, _: (greet(device), 0)[1], 0)

    for copy in tables:
        copy.wait()
    my_row = me - band
    used = cnt_v[pl.ds(my_row, 1), :]
    listed = gcnt_v[...].reshape(1, n)
    blocks = ids_v[...]
    selected = sel_v[me]
    hit = jnp.zeros((list_len, n), jnp.float32)
    for c in range(cap):
        picked = jnp.where(c < used, selected[c:c + 1, :], -1)
        hit = jnp.where(blocks == picked, 1.0, hit)
    slots = lax.broadcasted_iota(jnp.int32, (list_len, n), 0)
    flags_v[...] = jnp.where(slots < listed, hit, 0.0)
    flag_copy = pltpu.make_async_copy(flags_v, flags, table_sem.at[0])
    flag_copy.start()

    @pl.when(owner)
    def _():
        lanes = lax.broadcasted_iota(jnp.int32, (n, cap, n), 2)
        for side in range(2):
            for_me = jnp.where(lanes == share + side, sel_v[...].astype(jnp.float32), 0.0)
            sender_blocks[side] = jnp.broadcast_to(
                jnp.sum(for_me, axis=2, keepdims=True), (n, cap, block_len)
            )

    for copy in first_loads:
        copy.wait()
    for copy in later_loads:
        copy.start()

    def pick_rows(o, _):
        rows = [pl.ds(sel_s[c, o], 1) for c in range(cap)]
        rows = [acc[row, :] + res_buf[row, :] for row in rows]
        count = cnt_s[my_row, o]
        for c in range(cap):
            outgoing[o, pl.ds(c, 1), :] = rows[c] * jnp.where(c < count, 1.0, 0.0)
        return 0

    lax.fori_loop(0, n, pick_rows, 0)

    def remote(source, target, phase, device):
        return pltpu.make_async_remote_copy(
            src_ref=source, dst_ref=target,
            send_sem=send_sems.at[phase], recv_sem=recv_sems.at[phase],
            device_id=(device,), device_id_type=MESH,
        )

    def arrived(part, phase):
        return remote(part, part, phase, lax.rem(me + 1, n))

    @pl.when(owner)
    def _():
        pl.semaphore_wait(barrier, n - 1)

    @pl.when(jnp.logical_not(owner))
    def _():
        pl.semaphore_wait(barrier, half)

    each_other(
        half,
        lambda device: remote(
            outgoing.at[pl.ds(2 * device, 2)], incoming.at[me], 0, device
        ).start(),
    )

    def dense_acc(i, _):
        rows = pl.ds(pl.multiple_of(i * chunk, chunk), chunk)
        acc[rows, :] = acc[rows, :] + res_buf[rows, :]
        return 0

    lax.fori_loop(0, block_count // chunk, dense_acc, 0)
    flag_copy.wait()

    def pick_kept(o, _):
        rows = [acc[pl.ds(ids[j, o], 1), :] for j in range(list_len)]
        for j in range(list_len):
            kept[o, pl.ds(j, 1), :] = rows[j] * (1.0 - flags[j, o])
        return 0

    lax.fori_loop(0, n, pick_kept, 0)
    for copy in later_loads:
        copy.wait()

    def pick_weights(o, _):
        blocks = [pl.ds(ids[j, o], 1) for j in range(list_len)]
        found = [(wts[block, :], mom[block, :]) for block in blocks]
        for j, (weight, moment) in enumerate(found):
            wrows[o, pl.ds(j, 1), :] = weight
            mrows[o, pl.ds(j, 1), :] = moment
        return 0

    lax.fori_loop(0, n, pick_weights, 0)

    def dense_step(i, _):
        rows = pl.ds(pl.multiple_of(i * chunk, chunk), chunk)
        decayed = momentum_coef * mom[rows, :]
        mom[rows, :] = decayed
        wts[rows, :] = wts[rows, :] - learning_rate * decayed
        return 0

    lax.fori_loop(0, block_count // chunk, dense_step, 0)

    @pl.when(owner)
    def _():
        incoming[me] = outgoing[pl.ds(share, 2)]
        arrived(incoming.at[pl.ds(0, n - 1)], 0).wait_recv()
        for side in range(2):
            listed_here = gcnt_s[share + side]
            rows = incoming[:, side]
            for j in range(list_len):
                block = jnp.where(j < listed_here, ids[j, share + side], -1).astype(jnp.float32)
                chosen = jnp.where(sender_blocks[side] == block, rows, 0.0)
                updates[share + side, pl.ds(j, 1), :] = jnp.sum(
                    jnp.sum(chosen, axis=0), axis=0, keepdims=True
                )
        own = updates.at[pl.ds(share, 2)]
        each_other(n, lambda device: remote(own, own, 1, device).start())
        arrived(outgoing.at[pl.ds(0, n - 2)], 0).wait_send()
        arrived(updates.at[pl.ds(0, n - 2)], 1).wait_recv()

    @pl.when(jnp.logical_not(owner))
    def _():
        arrived(outgoing, 0).wait_send()
        arrived(updates, 1).wait_recv()

    new_rows = momentum_coef * mrows[...] + updates[...]
    mrows[...] = new_rows
    wrows[...] = wrows[...] - learning_rate * new_rows

    @pl.when(owner)
    def _():
        for _ in range(2):
            arrived(updates.at[pl.ds(0, n - 1)], 1).wait_send()


def finish(
    ids, acc_in, mom_in, wts_in, kept, mrows, wrows,
    new_weights, new_momentum, new_residual, acc, mom, wts,
    sems,
):
    half, list_len = kept.shape[0] // 2, kept.shape[1]
    copies = []

    def place(*pairs):
        def step(c, _):
            places = [(side, j) for side in range(2) for j in range(list_len)]
            targets = [pl.ds(ids[j, 2 * c + side], 1) for side, j in places]
            for rows, whole in pairs:
                values = [rows[2 * c + side, pl.ds(j, 1), :] for side, j in places]
                for target, value in zip(targets, values):
                    whole[target, :] = value
            return 0

        lax.fori_loop(0, half, step, 0)

    def write(whole, result):
        copies.extend(pieces(whole, result, sems, len(copies)))
        for copy in copies[-PIECES:]:
            copy.start()

    place((kept, acc))
    write(acc, new_residual)
    place((mrows, mom), (wrows, wts))
    write(mom, new_momentum)
    write(wts, new_weights)
    for copy in copies:
        copy.wait()


def local(n, gradient, residual, weights, momentum, sel_idx, sel_count, gath_idx, gath_count):
    block_count, block_len = weights.shape
    cap, list_len = sel_idx.shape[2], gath_idx.shape[1]
    f32, i32 = jnp.float32, jnp.int32
    dense = pltpu.VMEM((block_count, block_len), f32)
    tiles = pltpu.VMEM((n, list_len, block_len), f32)
    picks = pltpu.VMEM((n, cap, block_len), f32)
    table = pltpu.SMEM((list_len, n), i32)
    hbm = pl.BlockSpec(memory_space=pltpu.HBM)
    vmem = pl.BlockSpec(memory_space=pltpu.VMEM)
    smem = pl.BlockSpec(memory_space=pltpu.SMEM)
    dense_bytes = block_count * block_len * 4
    tile_bytes = n * list_len * block_len * 4
    chunk = 256

    acc, mom, wts, kept, mrows, wrows, ids = pl.pallas_call(
        functools.partial(exchange, n, chunk),
        out_shape=(dense, dense, dense, tiles, tiles, tiles, table),
        in_specs=[hbm] * 8,
        out_specs=[vmem] * 6 + [smem],
        scratch_shapes=[
            dense,
            pltpu.SMEM((cap, n), i32),
            pltpu.SMEM((ROWS, n), i32),
            pltpu.SMEM((n,), i32),
            pltpu.SMEM((list_len, n), f32),
            pltpu.VMEM((n, cap, n), i32),
            pltpu.VMEM((ROWS, n), i32),
            pltpu.VMEM((n,), i32),
            pltpu.VMEM((list_len, n), i32),
            pltpu.VMEM((list_len, n), f32),
            picks,
            pltpu.VMEM((n, 2, cap, block_len), f32),
            pltpu.VMEM((2, n, cap, block_len), f32),
            tiles,
            pltpu.SemaphoreType.DMA((4 * PIECES,)),
            pltpu.SemaphoreType.DMA((8,)),
            pltpu.SemaphoreType.DMA((2,)),
            pltpu.SemaphoreType.DMA((2,)),
        ],
        compiler_params=pltpu.CompilerParams(
            collective_id=0, has_side_effects=True,
            vmem_limit_bytes=dense_bytes + 12 * tile_bytes + (1 << 21),
        ),
        cost_estimate=pl.CostEstimate(
            flops=5 * block_count * block_len, bytes_accessed=4 * dense_bytes, transcendentals=0
        ),
        name="exchange",
    )(*[
        pltpu.with_memory_space_constraint(operand, pltpu.HBM)
        for operand in (
            gradient.reshape(block_count, block_len),
            residual.reshape(block_count, block_len),
            weights,
            momentum,
            sel_idx.transpose(0, 2, 1),
            sel_count,
            gath_idx.T,
            gath_count,
        )
    ])
    whole = jax.ShapeDtypeStruct((block_count, block_len), f32)
    new_weights, new_momentum, new_residual, _, _, _ = pl.pallas_call(
        finish,
        out_shape=(whole, whole, whole, dense, dense, dense),
        in_specs=[smem] + [vmem] * 6,
        out_specs=[hbm] * 3 + [vmem] * 3,
        input_output_aliases={1: 3, 2: 4, 3: 5},
        scratch_shapes=[pltpu.SemaphoreType.DMA((3 * PIECES,))],
        compiler_params=pltpu.CompilerParams(vmem_limit_bytes=1 << 21),
        cost_estimate=pl.CostEstimate(flops=0, bytes_accessed=3 * dense_bytes, transcendentals=0),
        name="finish",
    )(ids, acc, mom, wts, kept, mrows, wrows)
    return new_weights, new_momentum, new_residual[None]


def solution(mesh):
    placed = (P("dp", None, None), P("dp", None, None), P(), P(), P(), P(), P(), P())
    return jax.shard_map(
        functools.partial(local, mesh.shape["dp"]),
        mesh=mesh,
        in_specs=placed,
        out_specs=(P(), P(), P("dp", None, None)),
        check_vma=False,
    )
```

```python
import functools

import jax
import jax.numpy as jnp
from jax import lax
from jax.experimental import pallas as pl
from jax.experimental.pallas import tpu as pltpu
from jax.sharding import PartitionSpec as P

MESH = pl.DeviceIdType.MESH
momentum_coef = 0.9
learning_rate = 0.05
ROWS = 8
PIECES = 2


def pieces(source, target, sems, first):
    rows = source.shape[0] // PIECES
    return [
        pltpu.make_async_copy(
            source.at[pl.ds(i * rows, rows)], target.at[pl.ds(i * rows, rows)], sems.at[first + i]
        )
        for i in range(PIECES)
    ]


def exchange(
    n, chunk,
    grad, resid, weights, momentum, sel, counts, lists, list_counts,
    acc, mom, wts, kept, mrows, wrows, ids,
    res_buf, sel_s, cnt_s, gcnt_s, flags, sel_v, cnt_v, gcnt_v, ids_v, flags_v,
    outgoing, incoming, sender_blocks, updates,
    load_sem, table_sem, send_sems, recv_sems,
):
    half = n // 2
    me = lax.axis_index("dp")
    cap, list_len = sel_s.shape[0], ids.shape[0]
    block_count, block_len = acc.shape

    band = pl.multiple_of((me // ROWS) * ROWS, ROWS)
    tables = [
        pltpu.make_async_copy(source, target, table_sem.at[i])
        for i, (source, target) in enumerate((
            (lists, ids), (sel.at[me], sel_s), (counts.at[pl.ds(band, ROWS)], cnt_s), (list_counts, gcnt_s),
            (sel, sel_v), (counts.at[pl.ds(band, ROWS)], cnt_v), (list_counts, gcnt_v), (lists, ids_v),
        ))
    ]

    def load(source, target, first):
        return pieces(source, target, load_sem, first)

    first_loads = load(grad, acc, 0) + load(resid, res_buf, PIECES)
    later_loads = load(momentum, mom, 2 * PIECES) + load(weights, wts, 3 * PIECES)
    for copy in tables[:4] + first_loads + tables[4:]:
        copy.start()

    owner = me < half
    quarter = half // 2
    core = me % 2
    sibling = me + 1 - 2 * core

    def share_of(device):
        return 2 * ((device % 2) * quarter + device // 2)

    share = share_of(me)

    def each_other(stop, act):
        def step(device, _):
            @pl.when(device != me)
            def _():
                act(device)
            return 0

        lax.fori_loop(0, stop, step, 0)

    barrier = pltpu.get_barrier_semaphore()

    def greet(device):
        pl.semaphore_signal(barrier, inc=1, device_id=(device,), device_id_type=MESH)

    each_other(half, greet)

    @pl.when(owner)
    def _():
        lax.fori_loop(half, n, lambda device, _: (greet(device), 0)[1], 0)

    @pl.when(jnp.logical_not(owner))
    def _():
        greet(sibling)

    for copy in tables:
        copy.wait()
    my_row = me - band
    used = cnt_v[pl.ds(my_row, 1), :]
    listed = gcnt_v[...].reshape(1, n)
    blocks = ids_v[...]
    selected = sel_v[me]
    hit = jnp.zeros((list_len, n), jnp.float32)
    for c in range(cap):
        picked = jnp.where(c < used, selected[c:c + 1, :], -1)
        hit = jnp.where(blocks == picked, 1.0, hit)
    slots = lax.broadcasted_iota(jnp.int32, (list_len, n), 0)
    flags_v[...] = jnp.where(slots < listed, hit, 0.0)
    flag_copy = pltpu.make_async_copy(flags_v, flags, table_sem.at[0])
    flag_copy.start()

    @pl.when(owner)
    def _():
        lanes = lax.broadcasted_iota(jnp.int32, (n, cap, n), 2)
        for side in range(2):
            for_me = jnp.where(lanes == share + side, sel_v[...].astype(jnp.float32), 0.0)
            sender_blocks[side] = jnp.broadcast_to(
                jnp.sum(for_me, axis=2, keepdims=True), (n, cap, block_len)
            )

    for copy in first_loads:
        copy.wait()
    for copy in later_loads:
        copy.start()

    def pick_rows(o, _):
        rows = [pl.ds(sel_s[c, o], 1) for c in range(cap)]
        rows = [acc[row, :] + res_buf[row, :] for row in rows]
        count = cnt_s[my_row, o]
        for c in range(cap):
            outgoing[o, pl.ds(c, 1), :] = rows[c] * jnp.where(c < count, 1.0, 0.0)
        return 0

    lax.fori_loop(0, n, pick_rows, 0)

    def remote(source, target, phase, device):
        return pltpu.make_async_remote_copy(
            src_ref=source, dst_ref=target,
            send_sem=send_sems.at[phase], recv_sem=recv_sems.at[phase],
            device_id=(device,), device_id_type=MESH,
        )

    def arrived(part, phase):
        return remote(part, part, phase, lax.rem(me + 1, n))

    @pl.when(owner)
    def _():
        pl.semaphore_wait(barrier, n - 1)

    @pl.when(jnp.logical_not(owner))
    def _():
        pl.semaphore_wait(barrier, half + 1)

    each_other(
        half,
        lambda device: remote(
            outgoing.at[pl.ds(share_of(device), 2)], incoming.at[me], 0, device
        ).start(),
    )

    def dense_acc(i, _):
        rows = pl.ds(pl.multiple_of(i * chunk, chunk), chunk)
        acc[rows, :] = acc[rows, :] + res_buf[rows, :]
        return 0

    lax.fori_loop(0, block_count // chunk, dense_acc, 0)
    flag_copy.wait()

    def pick_kept(o, _):
        rows = [acc[pl.ds(ids[j, o], 1), :] for j in range(list_len)]
        for j in range(list_len):
            kept[o, pl.ds(j, 1), :] = rows[j] * (1.0 - flags[j, o])
        return 0

    lax.fori_loop(0, n, pick_kept, 0)
    for copy in later_loads:
        copy.wait()

    def pick_weights(o, _):
        blocks = [pl.ds(ids[j, o], 1) for j in range(list_len)]
        found = [(wts[block, :], mom[block, :]) for block in blocks]
        for j, (weight, moment) in enumerate(found):
            wrows[o, pl.ds(j, 1), :] = weight
            mrows[o, pl.ds(j, 1), :] = moment
        return 0

    lax.fori_loop(0, n, pick_weights, 0)

    def dense_step(i, _):
        rows = pl.ds(pl.multiple_of(i * chunk, chunk), chunk)
        decayed = momentum_coef * mom[rows, :]
        mom[rows, :] = decayed
        wts[rows, :] = wts[rows, :] - learning_rate * decayed
        return 0

    lax.fori_loop(0, block_count // chunk, dense_step, 0)

    @pl.when(owner)
    def _():
        incoming[me] = outgoing[pl.ds(share, 2)]
        arrived(incoming.at[pl.ds(0, n - 1)], 0).wait_recv()
        for side in range(2):
            listed_here = gcnt_s[share + side]
            rows = incoming[:, side]
            for j in range(list_len):
                block = jnp.where(j < listed_here, ids[j, share + side], -1).astype(jnp.float32)
                chosen = jnp.where(sender_blocks[side] == block, rows, 0.0)
                updates[share + side, pl.ds(j, 1), :] = jnp.sum(
                    jnp.sum(chosen, axis=0), axis=0, keepdims=True
                )
        own = updates.at[pl.ds(share, 2)]
        each_other(half, lambda device: remote(own, own, 1, device).start())

        def send_up(i, _):
            remote(own, own, 1, half + 2 * i + core).start()
            return 0

        lax.fori_loop(0, quarter, send_up, 0)
        arrived(outgoing.at[pl.ds(0, n - 2)], 0).wait_send()
        arrived(updates.at[pl.ds(0, n - 2)], 1).wait_recv()

    @pl.when(jnp.logical_not(owner))
    def _():
        arrived(outgoing, 0).wait_send()
        here, there = updates.at[pl.ds(core * half, half)], updates.at[pl.ds((1 - core) * half, half)]
        arrived(here, 1).wait_recv()
        relay = remote(here, here, 2, sibling)
        relay.start()
        relay.wait_send()
        arrived(there, 2).wait_recv()

    new_rows = momentum_coef * mrows[...] + updates[...]
    mrows[...] = new_rows
    wrows[...] = wrows[...] - learning_rate * new_rows

    @pl.when(owner)
    def _():
        arrived(updates.at[pl.ds(0, n - 2)], 1).wait_send()
        arrived(updates.at[pl.ds(0, half)], 1).wait_send()


def finish(
    ids, acc_in, mom_in, wts_in, kept, mrows, wrows,
    new_weights, new_momentum, new_residual, acc, mom, wts,
    sems,
):
    half, list_len = kept.shape[0] // 2, kept.shape[1]
    copies = []

    def place(*pairs):
        def step(c, _):
            places = [(side, j) for side in range(2) for j in range(list_len)]
            targets = [pl.ds(ids[j, 2 * c + side], 1) for side, j in places]
            for rows, whole in pairs:
                values = [rows[2 * c + side, pl.ds(j, 1), :] for side, j in places]
                for target, value in zip(targets, values):
                    whole[target, :] = value
            return 0

        lax.fori_loop(0, half, step, 0)

    def write(whole, result):
        copies.extend(pieces(whole, result, sems, len(copies)))
        for copy in copies[-PIECES:]:
            copy.start()

    place((kept, acc))
    write(acc, new_residual)
    place((mrows, mom), (wrows, wts))
    write(mom, new_momentum)
    write(wts, new_weights)
    for copy in copies:
        copy.wait()


def local(n, gradient, residual, weights, momentum, sel_idx, sel_count, gath_idx, gath_count):
    block_count, block_len = weights.shape
    cap, list_len = sel_idx.shape[2], gath_idx.shape[1]
    f32, i32 = jnp.float32, jnp.int32
    dense = pltpu.VMEM((block_count, block_len), f32)
    tiles = pltpu.VMEM((n, list_len, block_len), f32)
    picks = pltpu.VMEM((n, cap, block_len), f32)
    table = pltpu.SMEM((list_len, n), i32)
    hbm = pl.BlockSpec(memory_space=pltpu.HBM)
    vmem = pl.BlockSpec(memory_space=pltpu.VMEM)
    smem = pl.BlockSpec(memory_space=pltpu.SMEM)
    dense_bytes = block_count * block_len * 4
    tile_bytes = n * list_len * block_len * 4
    chunk = 256

    acc, mom, wts, kept, mrows, wrows, ids = pl.pallas_call(
        functools.partial(exchange, n, chunk),
        out_shape=(dense, dense, dense, tiles, tiles, tiles, table),
        in_specs=[hbm] * 8,
        out_specs=[vmem] * 6 + [smem],
        scratch_shapes=[
            dense,
            pltpu.SMEM((cap, n), i32),
            pltpu.SMEM((ROWS, n), i32),
            pltpu.SMEM((n,), i32),
            pltpu.SMEM((list_len, n), f32),
            pltpu.VMEM((n, cap, n), i32),
            pltpu.VMEM((ROWS, n), i32),
            pltpu.VMEM((n,), i32),
            pltpu.VMEM((list_len, n), i32),
            pltpu.VMEM((list_len, n), f32),
            picks,
            pltpu.VMEM((n, 2, cap, block_len), f32),
            pltpu.VMEM((2, n, cap, block_len), f32),
            tiles,
            pltpu.SemaphoreType.DMA((4 * PIECES,)),
            pltpu.SemaphoreType.DMA((8,)),
            pltpu.SemaphoreType.DMA((3,)),
            pltpu.SemaphoreType.DMA((3,)),
        ],
        compiler_params=pltpu.CompilerParams(
            collective_id=0, has_side_effects=True,
            vmem_limit_bytes=dense_bytes + 12 * tile_bytes + (1 << 21),
        ),
        cost_estimate=pl.CostEstimate(
            flops=5 * block_count * block_len, bytes_accessed=4 * dense_bytes, transcendentals=0
        ),
        name="exchange",
    )(*[
        pltpu.with_memory_space_constraint(operand, pltpu.HBM)
        for operand in (
            gradient.reshape(block_count, block_len),
            residual.reshape(block_count, block_len),
            weights,
            momentum,
            sel_idx.transpose(0, 2, 1),
            sel_count,
            gath_idx.T,
            gath_count,
        )
    ])
    whole = jax.ShapeDtypeStruct((block_count, block_len), f32)
    new_weights, new_momentum, new_residual, _, _, _ = pl.pallas_call(
        finish,
        out_shape=(whole, whole, whole, dense, dense, dense),
        in_specs=[smem] + [vmem] * 6,
        out_specs=[hbm] * 3 + [vmem] * 3,
        input_output_aliases={1: 3, 2: 4, 3: 5},
        scratch_shapes=[pltpu.SemaphoreType.DMA((3 * PIECES,))],
        compiler_params=pltpu.CompilerParams(vmem_limit_bytes=1 << 21),
        cost_estimate=pl.CostEstimate(flops=0, bytes_accessed=3 * dense_bytes, transcendentals=0),
        name="finish",
    )(ids, acc, mom, wts, kept, mrows, wrows)
    return new_weights, new_momentum, new_residual[None]


def solution(mesh):
    placed = (P("dp", None, None), P("dp", None, None), P(), P(), P(), P(), P(), P())
    return jax.shard_map(
        functools.partial(local, mesh.shape["dp"]),
        mesh=mesh,
        in_specs=placed,
        out_specs=(P(), P(), P("dp", None, None)),
        check_vma=False,
    )
```

```python
import functools

import jax
import jax.numpy as jnp
from jax import lax
from jax.experimental import pallas as pl
from jax.experimental.pallas import tpu as pltpu
from jax.sharding import PartitionSpec as P

MESH = pl.DeviceIdType.MESH
momentum_coef = 0.9
learning_rate = 0.05
ROWS = 8
PIECES = 2


def pieces(source, target, sems, first):
    rows = source.shape[0] // PIECES
    return [
        pltpu.make_async_copy(
            source.at[pl.ds(i * rows, rows)], target.at[pl.ds(i * rows, rows)], sems.at[first + i]
        )
        for i in range(PIECES)
    ]


def exchange(
    n, chunk,
    grad, resid, weights, momentum, sel, counts, lists, list_counts,
    acc, mom, wts, kept, mrows, wrows, ids,
    res_buf, sel_s, cnt_s, gcnt_s, flags, sel_v, cnt_v, gcnt_v, ids_v, flags_v,
    outgoing, incoming, sender_blocks, updates,
    load_sem, table_sem, send_sems, recv_sems,
):
    half = n // 2
    me = lax.axis_index("dp")
    cap, list_len = sel_s.shape[0], ids.shape[0]
    block_count, block_len = acc.shape

    band = pl.multiple_of((me // ROWS) * ROWS, ROWS)
    tables = [
        pltpu.make_async_copy(source, target, table_sem.at[i])
        for i, (source, target) in enumerate((
            (lists, ids), (sel.at[me], sel_s), (counts.at[pl.ds(band, ROWS)], cnt_s), (list_counts, gcnt_s),
            (sel, sel_v), (counts.at[pl.ds(band, ROWS)], cnt_v), (list_counts, gcnt_v), (lists, ids_v),
        ))
    ]

    def load(source, target, first):
        return pieces(source, target, load_sem, first)

    first_loads = load(grad, acc, 0) + load(resid, res_buf, PIECES)
    later_loads = load(momentum, mom, 2 * PIECES) + load(weights, wts, 3 * PIECES)
    for copy in tables[:4] + first_loads + tables[4:]:
        copy.start()

    owner = me < half
    quarter = half // 2
    core = me % 2
    sibling = me + 1 - 2 * core

    def share_of(device):
        return 2 * ((device % 2) * quarter + device // 2)

    share = share_of(me)

    def each_other(stop, act):
        def step(device, _):
            @pl.when(device != me)
            def _():
                act(device)
            return 0

        lax.fori_loop(0, stop, step, 0)

    barrier = pltpu.get_barrier_semaphore()

    def greet(device):
        pl.semaphore_signal(barrier, inc=1, device_id=(device,), device_id_type=MESH)

    each_other(half, greet)

    @pl.when(owner)
    def _():
        lax.fori_loop(half, n, lambda device, _: (greet(device), 0)[1], 0)

    @pl.when(jnp.logical_not(owner))
    def _():
        greet(sibling)

    for copy in tables:
        copy.wait()
    my_row = me - band
    used = cnt_v[pl.ds(my_row, 1), :]
    listed = gcnt_v[...].reshape(1, n)
    blocks = ids_v[...]
    selected = sel_v[me]
    hit = jnp.zeros((list_len, n), jnp.float32)
    for c in range(cap):
        picked = jnp.where(c < used, selected[c:c + 1, :], -1)
        hit = jnp.where(blocks == picked, 1.0, hit)
    slots = lax.broadcasted_iota(jnp.int32, (list_len, n), 0)
    flags_v[...] = jnp.where(slots < listed, hit, 0.0)
    flag_copy = pltpu.make_async_copy(flags_v, flags, table_sem.at[0])
    flag_copy.start()

    @pl.when(owner)
    def _():
        lanes = lax.broadcasted_iota(jnp.int32, (n, cap, n), 2)
        for side in range(2):
            for_me = jnp.where(lanes == share + side, sel_v[...].astype(jnp.float32), 0.0)
            sender_blocks[side] = jnp.broadcast_to(
                jnp.sum(for_me, axis=2, keepdims=True), (n, cap, block_len)
            )

    for copy in first_loads:
        copy.wait()
    for copy in later_loads:
        copy.start()

    def pick_rows(o, _):
        rows = [pl.ds(sel_s[c, o], 1) for c in range(cap)]
        rows = [acc[row, :] + res_buf[row, :] for row in rows]
        count = cnt_s[my_row, o]
        for c in range(cap):
            outgoing[o, pl.ds(c, 1), :] = rows[c] * jnp.where(c < count, 1.0, 0.0)
        return 0

    lax.fori_loop(0, n, pick_rows, 0)

    def remote(source, target, phase, device):
        return pltpu.make_async_remote_copy(
            src_ref=source, dst_ref=target,
            send_sem=send_sems.at[phase], recv_sem=recv_sems.at[phase],
            device_id=(device,), device_id_type=MESH,
        )

    def arrived(part, phase):
        return remote(part, part, phase, lax.rem(me + 1, n))

    @pl.when(owner)
    def _():
        pl.semaphore_wait(barrier, n - 1)

    @pl.when(jnp.logical_not(owner))
    def _():
        pl.semaphore_wait(barrier, half + 1)

    each_other(
        half,
        lambda device: remote(
            outgoing.at[pl.ds(share_of(device), 2)], incoming.at[me], 0, device
        ).start(),
    )

    def dense_acc(i, _):
        rows = pl.ds(pl.multiple_of(i * chunk, chunk), chunk)
        acc[rows, :] = acc[rows, :] + res_buf[rows, :]
        return 0

    lax.fori_loop(0, block_count // chunk, dense_acc, 0)
    flag_copy.wait()

    def pick_kept(o, _):
        rows = [acc[pl.ds(ids[j, o], 1), :] for j in range(list_len)]
        for j in range(list_len):
            kept[o, pl.ds(j, 1), :] = rows[j] * (1.0 - flags[j, o])
        return 0

    lax.fori_loop(0, n, pick_kept, 0)
    for copy in later_loads:
        copy.wait()

    def pick_weights(o, _):
        blocks = [pl.ds(ids[j, o], 1) for j in range(list_len)]
        found = [(wts[block, :], mom[block, :]) for block in blocks]
        for j, (weight, moment) in enumerate(found):
            wrows[o, pl.ds(j, 1), :] = weight
            mrows[o, pl.ds(j, 1), :] = moment
        return 0

    lax.fori_loop(0, n, pick_weights, 0)

    def dense_step(i, _):
        rows = pl.ds(pl.multiple_of(i * chunk, chunk), chunk)
        decayed = momentum_coef * mom[rows, :]
        mom[rows, :] = decayed
        wts[rows, :] = wts[rows, :] - learning_rate * decayed
        return 0

    lax.fori_loop(0, block_count // chunk, dense_step, 0)

    @pl.when(owner)
    def _():
        incoming[me] = outgoing[pl.ds(share, 2)]
        arrived(incoming.at[pl.ds(0, n - 1)], 0).wait_recv()
        for side in range(2):
            listed_here = gcnt_s[share + side]
            rows = incoming[:, side]
            for j in range(list_len):
                block = jnp.where(j < listed_here, ids[j, share + side], -1).astype(jnp.float32)
                chosen = jnp.where(sender_blocks[side] == block, rows, 0.0)
                updates[share + side, pl.ds(j, 1), :] = jnp.sum(
                    jnp.sum(chosen, axis=0), axis=0, keepdims=True
                )
        own = updates.at[pl.ds(share, 2)]

        def send_up(i, _):
            remote(own, own, 1, n - 2 * i - 2 + core).start()
            return 0

        lax.fori_loop(0, quarter, send_up, 0)
        each_other(half, lambda device: remote(own, own, 1, device).start())
        arrived(outgoing.at[pl.ds(0, n - 2)], 0).wait_send()
        arrived(updates.at[pl.ds(0, n - 2)], 1).wait_recv()

    @pl.when(jnp.logical_not(owner))
    def _():
        arrived(outgoing, 0).wait_send()
        here, there = updates.at[pl.ds(core * half, half)], updates.at[pl.ds((1 - core) * half, half)]
        arrived(here, 1).wait_recv()
        relay = remote(here, here, 2, sibling)
        relay.start()
        relay.wait_send()
        arrived(there, 2).wait_recv()

    new_rows = momentum_coef * mrows[...] + updates[...]
    mrows[...] = new_rows
    wrows[...] = wrows[...] - learning_rate * new_rows

    @pl.when(owner)
    def _():
        arrived(updates.at[pl.ds(0, n - 2)], 1).wait_send()
        arrived(updates.at[pl.ds(0, half)], 1).wait_send()


def finish(
    ids, acc_in, mom_in, wts_in, kept, mrows, wrows,
    new_weights, new_momentum, new_residual, acc, mom, wts,
    sems,
):
    half, list_len = kept.shape[0] // 2, kept.shape[1]
    copies = []

    def place(*pairs):
        def step(c, _):
            places = [(side, j) for side in range(2) for j in range(list_len)]
            targets = [pl.ds(ids[j, 2 * c + side], 1) for side, j in places]
            for rows, whole in pairs:
                values = [rows[2 * c + side, pl.ds(j, 1), :] for side, j in places]
                for target, value in zip(targets, values):
                    whole[target, :] = value
            return 0

        lax.fori_loop(0, half, step, 0)

    def write(whole, result):
        copies.extend(pieces(whole, result, sems, len(copies)))
        for copy in copies[-PIECES:]:
            copy.start()

    place((kept, acc))
    write(acc, new_residual)
    place((mrows, mom), (wrows, wts))
    write(mom, new_momentum)
    write(wts, new_weights)
    for copy in copies:
        copy.wait()


def local(n, gradient, residual, weights, momentum, sel_idx, sel_count, gath_idx, gath_count):
    block_count, block_len = weights.shape
    cap, list_len = sel_idx.shape[2], gath_idx.shape[1]
    f32, i32 = jnp.float32, jnp.int32
    dense = pltpu.VMEM((block_count, block_len), f32)
    tiles = pltpu.VMEM((n, list_len, block_len), f32)
    picks = pltpu.VMEM((n, cap, block_len), f32)
    table = pltpu.SMEM((list_len, n), i32)
    hbm = pl.BlockSpec(memory_space=pltpu.HBM)
    vmem = pl.BlockSpec(memory_space=pltpu.VMEM)
    smem = pl.BlockSpec(memory_space=pltpu.SMEM)
    dense_bytes = block_count * block_len * 4
    tile_bytes = n * list_len * block_len * 4
    chunk = 256

    acc, mom, wts, kept, mrows, wrows, ids = pl.pallas_call(
        functools.partial(exchange, n, chunk),
        out_shape=(dense, dense, dense, tiles, tiles, tiles, table),
        in_specs=[hbm] * 8,
        out_specs=[vmem] * 6 + [smem],
        scratch_shapes=[
            dense,
            pltpu.SMEM((cap, n), i32),
            pltpu.SMEM((ROWS, n), i32),
            pltpu.SMEM((n,), i32),
            pltpu.SMEM((list_len, n), f32),
            pltpu.VMEM((n, cap, n), i32),
            pltpu.VMEM((ROWS, n), i32),
            pltpu.VMEM((n,), i32),
            pltpu.VMEM((list_len, n), i32),
            pltpu.VMEM((list_len, n), f32),
            picks,
            pltpu.VMEM((n, 2, cap, block_len), f32),
            pltpu.VMEM((2, n, cap, block_len), f32),
            tiles,
            pltpu.SemaphoreType.DMA((4 * PIECES,)),
            pltpu.SemaphoreType.DMA((8,)),
            pltpu.SemaphoreType.DMA((3,)),
            pltpu.SemaphoreType.DMA((3,)),
        ],
        compiler_params=pltpu.CompilerParams(
            collective_id=0, has_side_effects=True,
            vmem_limit_bytes=dense_bytes + 12 * tile_bytes + (1 << 21),
        ),
        cost_estimate=pl.CostEstimate(
            flops=5 * block_count * block_len, bytes_accessed=4 * dense_bytes, transcendentals=0
        ),
        name="exchange",
    )(*[
        pltpu.with_memory_space_constraint(operand, pltpu.HBM)
        for operand in (
            gradient.reshape(block_count, block_len),
            residual.reshape(block_count, block_len),
            weights,
            momentum,
            sel_idx.transpose(0, 2, 1),
            sel_count,
            gath_idx.T,
            gath_count,
        )
    ])
    whole = jax.ShapeDtypeStruct((block_count, block_len), f32)
    new_weights, new_momentum, new_residual, _, _, _ = pl.pallas_call(
        finish,
        out_shape=(whole, whole, whole, dense, dense, dense),
        in_specs=[smem] + [vmem] * 6,
        out_specs=[hbm] * 3 + [vmem] * 3,
        input_output_aliases={1: 3, 2: 4, 3: 5},
        scratch_shapes=[pltpu.SemaphoreType.DMA((3 * PIECES,))],
        compiler_params=pltpu.CompilerParams(vmem_limit_bytes=1 << 21),
        cost_estimate=pl.CostEstimate(flops=0, bytes_accessed=3 * dense_bytes, transcendentals=0),
        name="finish",
    )(ids, acc, mom, wts, kept, mrows, wrows)
    return new_weights, new_momentum, new_residual[None]


def solution(mesh):
    placed = (P("dp", None, None), P("dp", None, None), P(), P(), P(), P(), P(), P())
    return jax.shard_map(
        functools.partial(local, mesh.shape["dp"]),
        mesh=mesh,
        in_specs=placed,
        out_specs=(P(), P(), P("dp", None, None)),
        check_vma=False,
    )
```

```python
import functools

import jax
import jax.numpy as jnp
from jax import lax
from jax.experimental import pallas as pl
from jax.experimental.pallas import tpu as pltpu
from jax.sharding import PartitionSpec as P

MESH = pl.DeviceIdType.MESH
momentum_coef = 0.9
learning_rate = 0.05
ROWS = 8
PIECES = 2


def pieces(source, target, sems, first):
    rows = source.shape[0] // PIECES
    return [
        pltpu.make_async_copy(
            source.at[pl.ds(i * rows, rows)], target.at[pl.ds(i * rows, rows)], sems.at[first + i]
        )
        for i in range(PIECES)
    ]


def exchange(
    n, chunk,
    grad, resid, weights, momentum, sel, counts, lists, list_counts,
    acc, mom, wts, kept, mrows, wrows, ids,
    res_buf, sel_s, cnt_s, gcnt_s, flags, sel_v, cnt_v, gcnt_v, ids_v, flags_v,
    outgoing, incoming, sender_blocks, updates,
    load_sem, table_sem, send_sems, recv_sems,
):
    half = n // 2
    me = lax.axis_index("dp")
    cap, list_len = sel_s.shape[0], ids.shape[0]
    block_count, block_len = acc.shape

    band = pl.multiple_of((me // ROWS) * ROWS, ROWS)
    tables = [
        pltpu.make_async_copy(source, target, table_sem.at[i])
        for i, (source, target) in enumerate((
            (lists, ids), (sel.at[me], sel_s), (counts.at[pl.ds(band, ROWS)], cnt_s), (list_counts, gcnt_s),
            (sel, sel_v), (counts.at[pl.ds(band, ROWS)], cnt_v), (list_counts, gcnt_v), (lists, ids_v),
        ))
    ]

    def load(source, target, first):
        return pieces(source, target, load_sem, first)

    first_loads = load(grad, acc, 0) + load(resid, res_buf, PIECES)
    later_loads = load(momentum, mom, 2 * PIECES) + load(weights, wts, 3 * PIECES)
    for copy in tables[:4] + first_loads + tables[4:]:
        copy.start()

    owner = me < half
    quarter = half // 2
    core = me % 2
    sibling = me + 1 - 2 * core

    def share_of(device):
        return 2 * ((device % 2) * quarter + device // 2)

    share = share_of(me)

    def each_other(stop, act):
        def step(device, _):
            @pl.when(device != me)
            def _():
                act(device)
            return 0

        lax.fori_loop(0, stop, step, 0)

    barrier = pltpu.get_barrier_semaphore()

    def greet(device):
        pl.semaphore_signal(barrier, inc=1, device_id=(device,), device_id_type=MESH)

    each_other(half, greet)

    @pl.when(owner)
    def _():
        lax.fori_loop(half, n, lambda device, _: (greet(device), 0)[1], 0)

    @pl.when(jnp.logical_not(owner))
    def _():
        greet(sibling)

    for copy in tables:
        copy.wait()
    my_row = me - band
    used = cnt_v[pl.ds(my_row, 1), :]
    listed = gcnt_v[...].reshape(1, n)
    blocks = ids_v[...]
    selected = sel_v[me]
    hit = jnp.zeros((list_len, n), jnp.float32)
    for c in range(cap):
        picked = jnp.where(c < used, selected[c:c + 1, :], -1)
        hit = jnp.where(blocks == picked, 1.0, hit)
    slots = lax.broadcasted_iota(jnp.int32, (list_len, n), 0)
    flags_v[...] = jnp.where(slots < listed, hit, 0.0)
    flag_copy = pltpu.make_async_copy(flags_v, flags, table_sem.at[0])
    flag_copy.start()

    @pl.when(owner)
    def _():
        lanes = lax.broadcasted_iota(jnp.int32, (n, cap, n), 2)
        for side in range(2):
            for_me = jnp.where(lanes == share + side, sel_v[...].astype(jnp.float32), 0.0)
            sender_blocks[side] = jnp.broadcast_to(
                jnp.sum(for_me, axis=2, keepdims=True), (n, cap, block_len)
            )

    for copy in first_loads:
        copy.wait()
    for copy in later_loads:
        copy.start()

    def pick_rows(o, _):
        rows = [pl.ds(sel_s[c, o], 1) for c in range(cap)]
        rows = [acc[row, :] + res_buf[row, :] for row in rows]
        count = cnt_s[my_row, o]
        for c in range(cap):
            outgoing[o, pl.ds(c, 1), :] = rows[c] * jnp.where(c < count, 1.0, 0.0)
        return 0

    lax.fori_loop(0, n, pick_rows, 0)

    def remote(source, target, phase, device):
        return pltpu.make_async_remote_copy(
            src_ref=source, dst_ref=target,
            send_sem=send_sems.at[phase], recv_sem=recv_sems.at[phase],
            device_id=(device,), device_id_type=MESH,
        )

    def arrived(part, phase):
        return remote(part, part, phase, lax.rem(me + 1, n))

    @pl.when(owner)
    def _():
        pl.semaphore_wait(barrier, n - 1)

    @pl.when(jnp.logical_not(owner))
    def _():
        pl.semaphore_wait(barrier, half + 1)

    each_other(
        half,
        lambda device: remote(
            outgoing.at[pl.ds(share_of(device), 2)], incoming.at[me], 0, device
        ).start(),
    )

    def dense_acc(i, _):
        rows = pl.ds(pl.multiple_of(i * chunk, chunk), chunk)
        acc[rows, :] = acc[rows, :] + res_buf[rows, :]
        return 0

    lax.fori_loop(0, block_count // chunk, dense_acc, 0)
    flag_copy.wait()

    def pick_kept(o, _):
        rows = [acc[pl.ds(ids[j, o], 1), :] for j in range(list_len)]
        for j in range(list_len):
            kept[o, pl.ds(j, 1), :] = rows[j] * (1.0 - flags[j, o])
        return 0

    lax.fori_loop(0, n, pick_kept, 0)
    for copy in later_loads:
        copy.wait()

    def pick_weights(o, _):
        blocks = [pl.ds(ids[j, o], 1) for j in range(list_len)]
        found = [(wts[block, :], mom[block, :]) for block in blocks]
        for j, (weight, moment) in enumerate(found):
            wrows[o, pl.ds(j, 1), :] = weight
            mrows[o, pl.ds(j, 1), :] = moment
        return 0

    lax.fori_loop(0, n, pick_weights, 0)

    def dense_step(i, _):
        rows = pl.ds(pl.multiple_of(i * chunk, chunk), chunk)
        decayed = momentum_coef * mom[rows, :]
        mom[rows, :] = decayed
        wts[rows, :] = wts[rows, :] - learning_rate * decayed
        return 0

    lax.fori_loop(0, block_count // chunk, dense_step, 0)

    @pl.when(owner)
    def _():
        incoming[me] = outgoing[pl.ds(share, 2)]
        arrived(incoming.at[pl.ds(0, n - 1)], 0).wait_recv()
        for side in range(2):
            listed_here = gcnt_s[share + side]
            rows = incoming[:, side]
            for j in range(list_len):
                block = jnp.where(j < listed_here, ids[j, share + side], -1).astype(jnp.float32)
                chosen = jnp.where(sender_blocks[side] == block, rows, 0.0)
                updates[share + side, pl.ds(j, 1), :] = jnp.sum(
                    jnp.sum(chosen, axis=0), axis=0, keepdims=True
                )
        own = updates.at[pl.ds(share, 2)]

        def send_up(i, _):
            remote(own, own, 1, half + 2 * ((i + me // 2) % quarter) + core).start()
            return 0

        lax.fori_loop(0, quarter, send_up, 0)
        each_other(half, lambda device: remote(own, own, 1, device).start())
        arrived(outgoing.at[pl.ds(0, n - 2)], 0).wait_send()
        arrived(updates.at[pl.ds(0, n - 2)], 1).wait_recv()

    @pl.when(jnp.logical_not(owner))
    def _():
        arrived(outgoing, 0).wait_send()
        here, there = updates.at[pl.ds(core * half, half)], updates.at[pl.ds((1 - core) * half, half)]
        arrived(here, 1).wait_recv()
        relay = remote(here, here, 2, sibling)
        relay.start()
        relay.wait_send()
        arrived(there, 2).wait_recv()

    new_rows = momentum_coef * mrows[...] + updates[...]
    mrows[...] = new_rows
    wrows[...] = wrows[...] - learning_rate * new_rows

    @pl.when(owner)
    def _():
        arrived(updates.at[pl.ds(0, n - 2)], 1).wait_send()
        arrived(updates.at[pl.ds(0, half)], 1).wait_send()


def finish(
    ids, acc_in, mom_in, wts_in, kept, mrows, wrows,
    new_weights, new_momentum, new_residual, acc, mom, wts,
    sems,
):
    half, list_len = kept.shape[0] // 2, kept.shape[1]
    copies = []

    def place(*pairs):
        def step(c, _):
            places = [(side, j) for side in range(2) for j in range(list_len)]
            targets = [pl.ds(ids[j, 2 * c + side], 1) for side, j in places]
            for rows, whole in pairs:
                values = [rows[2 * c + side, pl.ds(j, 1), :] for side, j in places]
                for target, value in zip(targets, values):
                    whole[target, :] = value
            return 0

        lax.fori_loop(0, half, step, 0)

    def write(whole, result):
        copies.extend(pieces(whole, result, sems, len(copies)))
        for copy in copies[-PIECES:]:
            copy.start()

    place((kept, acc))
    write(acc, new_residual)
    place((mrows, mom), (wrows, wts))
    write(mom, new_momentum)
    write(wts, new_weights)
    for copy in copies:
        copy.wait()


def local(n, gradient, residual, weights, momentum, sel_idx, sel_count, gath_idx, gath_count):
    block_count, block_len = weights.shape
    cap, list_len = sel_idx.shape[2], gath_idx.shape[1]
    f32, i32 = jnp.float32, jnp.int32
    dense = pltpu.VMEM((block_count, block_len), f32)
    tiles = pltpu.VMEM((n, list_len, block_len), f32)
    picks = pltpu.VMEM((n, cap, block_len), f32)
    table = pltpu.SMEM((list_len, n), i32)
    hbm = pl.BlockSpec(memory_space=pltpu.HBM)
    vmem = pl.BlockSpec(memory_space=pltpu.VMEM)
    smem = pl.BlockSpec(memory_space=pltpu.SMEM)
    dense_bytes = block_count * block_len * 4
    tile_bytes = n * list_len * block_len * 4
    chunk = 256

    acc, mom, wts, kept, mrows, wrows, ids = pl.pallas_call(
        functools.partial(exchange, n, chunk),
        out_shape=(dense, dense, dense, tiles, tiles, tiles, table),
        in_specs=[hbm] * 8,
        out_specs=[vmem] * 6 + [smem],
        scratch_shapes=[
            dense,
            pltpu.SMEM((cap, n), i32),
            pltpu.SMEM((ROWS, n), i32),
            pltpu.SMEM((n,), i32),
            pltpu.SMEM((list_len, n), f32),
            pltpu.VMEM((n, cap, n), i32),
            pltpu.VMEM((ROWS, n), i32),
            pltpu.VMEM((n,), i32),
            pltpu.VMEM((list_len, n), i32),
            pltpu.VMEM((list_len, n), f32),
            picks,
            pltpu.VMEM((n, 2, cap, block_len), f32),
            pltpu.VMEM((2, n, cap, block_len), f32),
            tiles,
            pltpu.SemaphoreType.DMA((4 * PIECES,)),
            pltpu.SemaphoreType.DMA((8,)),
            pltpu.SemaphoreType.DMA((3,)),
            pltpu.SemaphoreType.DMA((3,)),
        ],
        compiler_params=pltpu.CompilerParams(
            collective_id=0, has_side_effects=True,
            vmem_limit_bytes=dense_bytes + 12 * tile_bytes + (1 << 21),
        ),
        cost_estimate=pl.CostEstimate(
            flops=5 * block_count * block_len, bytes_accessed=4 * dense_bytes, transcendentals=0
        ),
        name="exchange",
    )(*[
        pltpu.with_memory_space_constraint(operand, pltpu.HBM)
        for operand in (
            gradient.reshape(block_count, block_len),
            residual.reshape(block_count, block_len),
            weights,
            momentum,
            sel_idx.transpose(0, 2, 1),
            sel_count,
            gath_idx.T,
            gath_count,
        )
    ])
    whole = jax.ShapeDtypeStruct((block_count, block_len), f32)
    new_weights, new_momentum, new_residual, _, _, _ = pl.pallas_call(
        finish,
        out_shape=(whole, whole, whole, dense, dense, dense),
        in_specs=[smem] + [vmem] * 6,
        out_specs=[hbm] * 3 + [vmem] * 3,
        input_output_aliases={1: 3, 2: 4, 3: 5},
        scratch_shapes=[pltpu.SemaphoreType.DMA((3 * PIECES,))],
        compiler_params=pltpu.CompilerParams(vmem_limit_bytes=1 << 21),
        cost_estimate=pl.CostEstimate(flops=0, bytes_accessed=3 * dense_bytes, transcendentals=0),
        name="finish",
    )(ids, acc, mom, wts, kept, mrows, wrows)
    return new_weights, new_momentum, new_residual[None]


def solution(mesh):
    placed = (P("dp", None, None), P("dp", None, None), P(), P(), P(), P(), P(), P())
    return jax.shard_map(
        functools.partial(local, mesh.shape["dp"]),
        mesh=mesh,
        in_specs=placed,
        out_specs=(P(), P(), P("dp", None, None)),
        check_vma=False,
    )
```
